256 devices in a mesh: group: 32 (over x, z_hi, core), member: 8 (over z_lo, y).
Axes of the slice: x: 4, y: 4, z: 8 (z_hi: 4, z_lo: 2; z = z_hi * 2 + z_lo), core: 2. Of those that a mesh axis runs over, the one named last changes fastest.
Arguments:
- picture_vectors: bfloat16 [32768, 1152], P(('group', 'member')), may hold values from -1.5 to 1.5
- caption_vectors: bfloat16 [32768, 1152], P(('group', 'member')), may hold values from -1.5 to 1.5
- logit_multiplier: float32 [1], replicated, may hold values from 4 to 16
- logit_offset: float32 [1], replicated, may hold values from -2 to 0
- partner_xor_codes: int32 [4], replicated, may hold values from 1 to 31, as said below
Outputs:
- grad_image: float32 [32768, 1152], P(('group', 'member'))
- text_embedding_gradient: float32 [32768, 1152], P(('group', 'member'))
The draws below stay inside these ranges and needn't reach their ends.
Inputs may be any that keep to these rules, and one draw needn't show every extreme that they name: `partner_xor_codes`: 4 distinct values; 1 and 31 are always among them.
All inputs are finite; a program needn't handle non-finite values.
Results may differ from the reference program's by a relative error of at most 0.0047.
Values may be sent and summed in bfloat16 or wider, within the bound.
A program may use at most 128 MiB of HBM per device.

```python
import math
import jax
import jax.numpy as jnp
from jax import lax

D = 1152
ROUNDS = 4
GROUPS = 32
PAIRS_PER_GROUP = 1024
BATCH = 32768


def draw_partner_xor_codes(key, part):
    key = jax.random.fold_in(key, 7)
    first_key, second_key = jax.random.split(key)
    middle = jax.random.permutation(first_key, GROUPS - 3) + 2
    chosen = jnp.concatenate([jnp.array([1, GROUPS - 1], jnp.int32), middle[:ROUNDS - 2].astype(jnp.int32)])
    return jax.random.permutation(second_key, chosen).astype(jnp.int32)


def block_levels(rng, extent, pieces, smallest, high):
    loudness, own = 1.0, jax.random.fold_in(rng, 6)
    for axis_at, shards_of in pieces:
        steps = jnp.exp(jax.random.uniform(jax.random.fold_in(own, axis_at), (shards_of,), jnp.float32, smallest / len(pieces), high / len(pieces)))
        loudness = loudness * jnp.repeat(steps, extent[axis_at] // shards_of).reshape([-1 if axis == axis_at else 1 for axis in range(len(extent))])
    return loudness


def noise(stream_key, dims, spread, most, cuts=(), held_as=jnp.bfloat16):
    gain = block_levels(stream_key, dims, cuts, -0.22, 0.18) if cuts else 1.0
    values = jax.random.normal(stream_key, dims, jnp.float32) * spread * gain
    return jnp.minimum(jnp.maximum(values, -most), most).astype(held_as)


def setup_inputs(seed: int = 0) -> dict:
    arg_keys = jax.random.split(jax.random.key(seed), 6)
    picture_vectors = noise(arg_keys[0], (BATCH, D), 0.25, 1.5, ((0, 256),))
    caption_vectors = noise(arg_keys[1], (BATCH, D), 0.25, 1.5, ((0, 256),))
    logit_multiplier = jnp.clip(jnp.exp(jax.random.uniform(arg_keys[2], (1,), jnp.float32, math.log(4.0), math.log(16.0))), 4.0, 16.0)
    logit_offset = jnp.clip(jax.random.uniform(arg_keys[3], (1,), jnp.float32, -2.0, 0.0), -2.0, 0.0)
    partner_xor_codes = draw_partner_xor_codes(jax.random.fold_in(arg_keys[5], 71), 0)
    return dict(picture_vectors=picture_vectors, caption_vectors=caption_vectors, logit_multiplier=logit_multiplier, logit_offset=logit_offset, partner_xor_codes=partner_xor_codes)


EPSILON = 1e-06

def normalized_rows(rows_in):
    values = rows_in.astype(jnp.float32)
    scale = lax.rsqrt(lax.optimization_barrier(jnp.sum(values * values, axis=-1, keepdims=True)) + EPSILON)
    return (values * scale, scale)

def back_unit(unit, scale, grad):
    return (grad - unit * lax.optimization_barrier(jnp.sum(unit * grad, axis=-1, keepdims=True))) * scale

def reference(picture_vectors, caption_vectors, logit_multiplier, logit_offset, partner_xor_codes):
    unit_u, norm_u = normalized_rows(picture_vectors)
    unit_v, norm_v = normalized_rows(caption_vectors)
    image_b = unit_u.astype(jnp.bfloat16)
    caption_sample_count = unit_v.astype(jnp.bfloat16)
    image_blocks = image_b.reshape(GROUPS, PAIRS_PER_GROUP, D)
    text_blocks = caption_sample_count.reshape(GROUPS, PAIRS_PER_GROUP, D)
    multiplier_single = logit_multiplier[0]
    offset_amount = logit_offset[0]
    round_mask_stack = jnp.concatenate([jnp.zeros((1,), jnp.int32), partner_xor_codes.astype(jnp.int32)])
    unit_diagonal_square = (jnp.arange(PAIRS_PER_GROUP, dtype=jnp.int32)[:, None] == jnp.arange(PAIRS_PER_GROUP, dtype=jnp.int32)[None, :]).astype(jnp.float32)

    def weights(left_operand, right_operand, positive_indicator):
        similarity_logits = lax.dot_general(left_operand, right_operand, (((1,), (1,)), ((), ())), preferred_element_type=jnp.float32)
        multiplier_factor = jax.nn.sigmoid(multiplier_single * similarity_logits + offset_amount) - positive_indicator * unit_diagonal_square
        return (multiplier_single * multiplier_factor).astype(jnp.bfloat16)

    def image_grad(group_id):
        left_operand = lax.dynamic_index_in_dim(image_blocks, group_id, 0, keepdims=False)
        total = jnp.zeros((PAIRS_PER_GROUP, D), jnp.float32)
        for round_id in range(ROUNDS + 1):
            partner = jnp.bitwise_xor(group_id, round_mask_stack[round_id])
            right_operand = lax.dynamic_index_in_dim(text_blocks, partner, 0, keepdims=False)
            positive_indicator = (round_mask_stack[round_id] == 0).astype(jnp.float32)
            block = weights(left_operand, right_operand, positive_indicator)
            total = total + jnp.dot(block, right_operand, preferred_element_type=jnp.float32)
        return total

    def text_grad(group_id):
        right_operand = lax.dynamic_index_in_dim(text_blocks, group_id, 0, keepdims=False)
        total = jnp.zeros((PAIRS_PER_GROUP, D), jnp.float32)
        for round_id in range(ROUNDS + 1):
            partner = jnp.bitwise_xor(group_id, round_mask_stack[round_id])
            left_operand = lax.dynamic_index_in_dim(image_blocks, partner, 0, keepdims=False)
            positive_indicator = (round_mask_stack[round_id] == 0).astype(jnp.float32)
            block = weights(left_operand, right_operand, positive_indicator)
            total = total + lax.dot_general(block, left_operand, (((0,), (0,)), ((), ())), preferred_element_type=jnp.float32)
        return total
    group_ids = jnp.arange(GROUPS, dtype=jnp.int32)
    d_u = lax.map(image_grad, group_ids).reshape(BATCH, D)
    d_v = lax.map(text_grad, group_ids).reshape(BATCH, D)
    return (back_unit(unit_u, norm_u, d_u), back_unit(unit_v, norm_v, d_v))
```

```python
import jax
import jax.numpy as jnp
from jax import lax
from jax.experimental import pallas as pl
from jax.experimental.pallas import tpu as pltpu
from jax.sharding import PartitionSpec as P

EPSILON = 1e-06
MESH = pl.DeviceIdType.MESH
BF = jnp.bfloat16
F32 = jnp.float32
WHOLE = (("group", "member"), None)
PARTS = 4
OWN, LO, Y1, Y3, LO_Y1, LO_Y3, Y2, LO_Y2 = range(8)


def flip(value, code):
    if code == 0:
        return value
    if code == 1:
        return value + 1 - 2 * (value % 2)
    if code == 2:
        return (value + 2) % 4
    return 3 - value


def peer(x=0, z=0, core=0, lo=0, y=0):
    group, member = lax.axis_index("group"), lax.axis_index("member")
    at_x, at_z, at_core = group // 8, (group // 2) % 4, group % 2
    at_lo, at_y = member // 4, member % 4
    return (
        flip(at_x, x) * 8 + flip(at_z, z) * 2 + flip(at_core, core),
        flip(at_lo, lo) * 4 + flip(at_y, y),
    )


PEERS = (
    dict(core=1),
    dict(x=1),
    dict(x=3),
    dict(x=3, core=1),
    dict(z=1),
    dict(z=3),
    dict(lo=1),
    dict(y=1),
    dict(y=3),
)


def unit_rows(raw):
    values = raw.astype(F32)
    scale = lax.rsqrt(jnp.sum(values * values, axis=-1, keepdims=True) + EPSILON)
    return values * scale, scale


def back_unit(unit, scale, grad):
    return (grad - unit * jnp.sum(unit * grad, axis=-1, keepdims=True)) * scale


def choose(code, zero, one, two, three):
    low = jnp.where(code == 1, one, zero)
    high = jnp.where(code == 3, three, two)
    return jnp.where(code >= 2, high, low)


def scratch(rows, wide):
    piece = rows // PARTS
    half = piece // 2
    unit = pltpu.VMEM((rows, wide), BF)
    both = pltpu.VMEM((2 * half, wide), BF)
    pair = pltpu.VMEM((2 * piece, wide), BF)
    each = lambda ref: [ref] * PARTS
    return dict(
        img=pltpu.VMEM((8 * rows, wide), BF),
        txt=pltpu.VMEM((5 * rows, wide), BF),
        wgt=pltpu.VMEM((5 * rows, 8 * rows), BF),
        bank=each(pltpu.VMEM((8, piece, wide), BF)),
        g_near=each(both),
        g_far=each(both),
        g_s3=each(both),
        g_s21=each(both),
        g_s23=each(both),
        g_r11=each(both),
        g_r13=each(both),
        g_r21=each(both),
        g_r23=each(both),
        d_own=each(pair),
        d_core=each(pair),
        b_near=each(both),
        b_far=each(both),
        b_s3=each(both),
        b_s21=each(both),
        b_s23=each(both),
        b_r11=each(both),
        b_r13=each(both),
        b_r21=each(both),
        b_r23=each(both),
        d31_out=each(pltpu.VMEM((piece, wide), BF)),
        d31_in=each(pltpu.VMEM((piece, wide), BF)),
        z_sum=each(pltpu.VMEM((4, piece, wide), F32)),
        z_s=each(pltpu.VMEM((3, piece, wide), BF)),
        z_r2=each(pltpu.VMEM((piece, wide), BF)),
        z_r1=each(pltpu.VMEM((piece, wide), BF)),
        z_r3=each(pltpu.VMEM((piece, wide), BF)),
        d_text=pltpu.VMEM((2 * rows, wide), F32),
        d_text_in=pltpu.VMEM((rows, wide), F32),
        d_img=pltpu.VMEM((8 * rows, wide), F32),
        i_s=[unit] * 7,
        i_r=[unit] * 7,
        scale_u=pltpu.VMEM((rows, 1), F32),
        scale_v=pltpu.VMEM((rows, 1), F32),
        send=pltpu.SemaphoreType.DMA((160,)),
        recv=pltpu.SemaphoreType.DMA((160,)),
    )


def kernel(pic_ref, cap_ref, mult_ref, off_ref, code_ref, gi_ref, gt_ref, s):
    rows, wide = pic_ref.shape
    piece = rows // PARTS
    half = piece // 2
    img, txt, wgt = s["img"], s["txt"], s["wgt"]
    copies = {}

    def send(name, src, dst, **to):
        at = len(copies)
        copy = pltpu.make_async_remote_copy(
            src_ref=src,
            dst_ref=dst,
            send_sem=s["send"].at[at],
            recv_sem=s["recv"].at[at],
            device_id=peer(**to),
            device_id_type=MESH,
        )
        copies[name] = copy
        copy.start()

    def arrived(*names):
        for name in names:
            copies[name].wait_recv()

    def slot(at):
        return pl.ds(at * rows, rows)

    def part(j):
        return pl.ds(j * piece, piece)

    barrier = pltpu.get_barrier_semaphore()
    for to in PEERS:
        pl.semaphore_signal(barrier, inc=1, device_id=peer(**to), device_id_type=MESH)

    mult, off = mult_ref[0], off_ref[0]
    codes = [code_ref[i] for i in range(4)]
    code_a, code_b = jnp.int32(99), jnp.int32(-1)
    for code in codes:
        code_a = jnp.minimum(code_a, jnp.where(code == 1, 99, code))
        code_b = jnp.maximum(code_b, jnp.where(code == 31, -1, code))
    core_of = [code_a & 1, code_b & 1]
    z_of = [(code_a >> 1) & 3, (code_b >> 1) & 3]
    x_of = [(code_a >> 3) & 3, (code_b >> 3) & 3]

    unit_v, scale_v = unit_rows(cap_ref[...])
    s["scale_v"][...] = scale_v
    own_text = unit_v.astype(BF)
    txt[slot(0), :] = own_text
    for j in range(PARTS):
        s["bank"][j][0] = own_text[j * piece : (j + 1) * piece]
    unit_u, scale_u = unit_rows(pic_ref[...])
    s["scale_u"][...] = scale_u
    img[slot(OWN), :] = unit_u.astype(BF)
    pl.semaphore_wait(barrier, len(PEERS))

    def z_first(j):
        src = s["bank"][j].at[0]
        send(f"z1_{j}", src, s["bank"][j].at[1], z=1)
        send(f"z3_{j}", src, s["bank"][j].at[3], z=3)

    def z_second(j):
        bank = s["bank"][j]
        near, far = pl.ds(0, half), pl.ds(half, half)
        arrived(f"z1_{j}")
        send(f"z2a_{j}", bank.at[1, near], bank.at[2, near], z=3)
        arrived(f"z3_{j}")
        send(f"z2b_{j}", bank.at[3, far], bank.at[2, far], z=1)
        send(f"t31_{j}", bank.at[3], txt.at[pl.ds(2 * rows + j * piece, piece)], x=3, core=1)
        send(f"c1_{j}", bank.at[1], bank.at[5], core=1)
        send(f"c3_{j}", bank.at[3], bank.at[7], core=1)

    def z_done(j):
        bank = s["bank"][j]
        arrived(f"z2a_{j}", f"z2b_{j}")
        send(f"c2_{j}", bank.at[2], bank.at[6], core=1)

    def x_send(tag, j, far, where):
        near_ref, far_ref, s3 = s[tag + "near"][j], s[tag + "far"][j], s[tag + "s3"][j]
        send(f"{tag}11_{j}", near_ref, s[tag + "r11"][j], x=1)
        for m in range(2):
            at = pl.ds(m * half, half)
            s3[at, :] = jnp.where(x_of[m] == 2, far_ref[at, :], near_ref[at, :])
        send(f"{tag}13_{j}", s3, s[tag + "r13"][j], x=3)

    def x_second(tag, j):
        far_ref = s[tag + "far"][j]
        for side, name in ((3, "11"), (1, "13")):
            arrived(f"{tag}{name}_{j}")
            got, out = s[f"{tag}r{name}"][j], s[f"{tag}s2{side}"][j]
            for m in range(2):
                at = pl.ds(m * half, half)
                out[at, :] = jnp.where(x_of[m] == 2, got[at, :], far_ref[at, :])
            send(f"{tag}2{side}_{j}", out, s[f"{tag}r2{side}"][j], x=side)

    def x_done(tag, j, m):
        at = pl.ds(m * half, half)
        r11, r13, r21, r23 = (s[f"{tag}r{n}"][j][at, :] for n in ("11", "13", "21", "23"))
        near = choose(x_of[m], s[tag + "near"][j][at, :], r11, r23, r13)
        far = choose(x_of[m], s[tag + "far"][j][at, :], r21, r21, r23)
        return near, far

    def x_text(j):
        bank = s["bank"][j]
        arrived(f"c1_{j}", f"c2_{j}", f"c3_{j}")
        for m in range(2):
            at = pl.ds(m * half, half)
            picked = bank[core_of[m] * 4 + z_of[m]]
            s["g_near"][j][at, :] = picked[:half]
            s["g_far"][j][at, :] = picked[half:]
        x_send("g_", j, None, None)

    def text_in(j):
        arrived(f"g_21_{j}", f"g_23_{j}")
        for m in range(2):
            near, far = x_done("g_", j, m)
            base = 3 * rows + (2 * j + m) * piece
            txt[pl.ds(base, half), :] = near
            txt[pl.ds(base + half, half), :] = far

    def weigh(start, count, positive):
        def tile(i, carry):
            cols = pl.ds(pl.multiple_of(i * 2 * rows, 2 * rows), 2 * rows)
            logits = lax.dot_general(
                txt[pl.ds(start, count), :],
                img[cols, :],
                (((1,), (1,)), ((), ())),
                preferred_element_type=F32,
            )
            factor = jax.nn.sigmoid(mult * logits + off)
            if positive:
                row = lax.broadcasted_iota(jnp.int32, factor.shape, 0)
                col = lax.broadcasted_iota(jnp.int32, factor.shape, 1) + i * 2 * rows
                factor = factor - jnp.where((row == col) & (row < rows), 1.0, 0.0)
            wgt[pl.ds(start, count), cols] = (mult * factor).astype(BF)
            return carry

        lax.fori_loop(0, 4, tile, 0)

    def text_grad(start, count):
        return jnp.dot(wgt[pl.ds(start, count), :], img[...], preferred_element_type=F32)

    def image_grad(start, count, at):
        cols = pl.ds(at * rows, 2 * rows)
        return lax.dot_general(
            wgt[pl.ds(start, count), cols],
            txt[pl.ds(start, count), :],
            (((0,), (0,)), ((), ())),
            preferred_element_type=F32,
        )

    def grads_out(j):
        start = 3 * rows + 2 * j * piece
        weigh(start, 2 * piece, False)
        s["d_own"][j][...] = text_grad(start, 2 * piece).astype(BF)
        send(f"dc_{j}", s["d_own"][j], s["d_core"][j], core=1)

    def grads_x(j):
        arrived(f"dc_{j}")
        own, other = s["d_own"][j], s["d_core"][j]
        for m in range(2):
            at = pl.ds(m * half, half)
            for name, base in (("near", m * piece), ("far", m * piece + half)):
                take = pl.ds(base, half)
                s["b_" + name][j][at, :] = jnp.where(core_of[m] == 1, other[take, :], own[take, :])
        x_send("b_", j, None, None)

    def grads_z(j):
        arrived(f"b_21_{j}", f"b_23_{j}", f"d31_{j}")
        total = s["z_sum"][j]
        zero = jnp.zeros((half, wide), F32)
        got = [x_done("b_", j, m) for m in range(2)]
        for h in range(2):
            at = pl.ds(h * half, half)
            a, b = got[0][h].astype(F32), got[1][h].astype(F32)
            for k in range(4):
                value = jnp.where(z_of[0] == k, a, zero) + jnp.where(z_of[1] == k, b, zero)
                if k == 3:
                    value = value + s["d31_in"][j][at, :].astype(F32)
                total[k, at, :] = value
        out = s["z_s"][j]
        out[0] = total[2].astype(BF)
        near, far = pl.ds(0, half), pl.ds(half, half)
        send(f"dz2a_{j}", out.at[0, near], s["z_r2"][j].at[near], z=3)
        send(f"dz2b_{j}", out.at[0, far], s["z_r2"][j].at[far], z=1)

    def grads_z_second(j):
        total, out, got = s["z_sum"][j], s["z_s"][j], s["z_r2"][j]
        near, far = pl.ds(0, half), pl.ds(half, half)
        arrived(f"dz2a_{j}")
        out[1, far, :] = total[1, far, :].astype(BF)
        out[1, near, :] = (total[1, near, :] + got[near, :].astype(F32)).astype(BF)
        send(f"dz1_{j}", out.at[1], s["z_r1"][j], z=1)
        arrived(f"dz2b_{j}")
        out[2, near, :] = total[3, near, :].astype(BF)
        out[2, far, :] = (total[3, far, :] + got[far, :].astype(F32)).astype(BF)
        send(f"dz3_{j}", out.at[2], s["z_r3"][j], z=3)

    def text_out(j):
        arrived(f"dz1_{j}", f"dz3_{j}")
        total = s["z_sum"][j][0] + s["z_r1"][j][...].astype(F32) + s["z_r3"][j][...].astype(F32)
        total = total + s["d_text"][part(j), :] + s["d_text_in"][part(j), :]
        scale = s["scale_v"][part(j), :]
        unit = cap_ref[part(j), :].astype(F32) * scale
        gt_ref[part(j), :] = back_unit(unit, scale, total)

    def early():
        weigh(0, 2 * rows, True)
        s["d_text"][...] = text_grad(0, 2 * rows)
        send("d1", s["d_text"].at[slot(1)], s["d_text_in"], core=1)

    def early31():
        weigh(2 * rows, rows, False)
        grad = text_grad(2 * rows, rows).astype(BF)
        for j in range(PARTS):
            s["d31_out"][j][...] = grad[j * piece : (j + 1) * piece]
            send(f"d31_{j}", s["d31_out"][j], s["d31_in"][j], x=3, core=1)

    def early_image():
        def tile(i, carry):
            at = pl.ds(pl.multiple_of(i * 2 * rows, 2 * rows), 2 * rows)
            s["d_img"][at, :] = lax.dot_general(
                wgt[pl.ds(0, 3 * rows), at],
                txt[pl.ds(0, 3 * rows), :],
                (((0,), (0,)), ((), ())),
                preferred_element_type=F32,
            )
            return carry

        lax.fori_loop(0, 4, tile, 0)

    def late_image(at):
        here = pl.ds(at * rows, 2 * rows)
        s["d_img"][here, :] = s["d_img"][here, :] + image_grad(3 * rows, 2 * rows, at)

    def image_send(name, n, value, **to):
        s["i_s"][n][...] = value.astype(BF)
        send(name, s["i_s"][n], s["i_r"][n], **to)

    def grad_of(at):
        return s["d_img"][slot(at), :]

    def got(n):
        return s["i_r"][n][...].astype(F32)

    def image_first():
        late_image(Y2)
        image_send("u7", 0, grad_of(LO_Y2), y=1)
        image_send("u6", 1, grad_of(Y2), y=3)
        late_image(LO_Y1)
        image_send("u4", 2, grad_of(LO_Y1), y=1)
        late_image(Y1)
        image_send("u3", 3, grad_of(Y3), y=3)
        late_image(OWN)

    def image_second():
        arrived("u7")
        image_send("u5", 4, grad_of(LO_Y3) + got(0), y=3)
        arrived("u6")
        image_send("u2", 5, grad_of(Y1) + got(1), y=1)

    def image_third():
        arrived("u4", "u5")
        image_send("ul", 6, grad_of(LO) + got(2) + got(4), lo=1)

    def image_out():
        arrived("u2", "u3", "ul")
        total = grad_of(OWN) + got(5) + got(3) + got(6)
        scale = s["scale_u"][...]
        unit = pic_ref[...].astype(F32) * scale
        gi_ref[...] = back_unit(unit, scale, total)

    send("l", img.at[slot(OWN)], img.at[slot(LO)], lo=1)
    z_first(0)
    send("y1", img.at[slot(OWN)], img.at[slot(Y1)], y=1)
    send("y3", img.at[slot(OWN)], img.at[slot(Y3)], y=3)
    send("t1", txt.at[slot(0)], txt.at[slot(1)], core=1)
    z_first(1)
    arrived("t1")
    for j in range(PARTS):
        s["bank"][j][4] = txt[pl.ds(rows + j * piece, piece), :]

    def image_lo():
        arrived("l")
        send("ly1", img.at[slot(LO)], img.at[slot(LO_Y1)], y=1)
        send("ly3", img.at[slot(LO)], img.at[slot(LO_Y3)], y=3)

    def image_y2():
        arrived("y1")
        send("y2", img.at[slot(Y1)], img.at[slot(Y2)], y=3)

    def image_lo_y2():
        arrived("ly3")
        send("ly2", img.at[slot(LO_Y3)], img.at[slot(LO_Y2)], y=1)

    z_second(0)
    z_first(2)
    image_lo()
    z_done(0)
    x_text(0)
    z_second(1)
    z_first(3)
    image_y2()
    x_second("g_", 0)
    z_done(1)
    x_text(1)
    text_in(0)
    z_second(2)
    image_lo_y2()
    x_second("g_", 1)
    z_done(2)
    x_text(2)
    text_in(1)
    z_second(3)
    arrived("y3", "ly1", "y2", "ly2")
    early()
    x_second("g_", 2)
    z_done(3)
    x_text(3)
    grads_out(0)
    arrived(*(f"t31_{j}" for j in range(PARTS)))
    early31()
    text_in(2)
    grads_x(0)
    x_second("g_", 3)
    grads_out(1)
    early_image()
    x_second("b_", 0)
    grads_x(1)
    grads_out(2)
    grads_z(0)
    text_in(3)
    grads_out(3)
    x_second("b_", 1)
    grads_x(2)
    image_first()
    grads_z_second(0)
    grads_x(3)
    x_second("b_", 2)
    grads_z(1)
    image_second()
    x_second("b_", 3)
    grads_z_second(1)
    grads_z(2)
    grads_z_second(2)
    grads_z(3)
    arrived("d1")
    text_out(0)
    image_third()
    grads_z_second(3)
    text_out(1)
    text_out(2)
    image_out()
    text_out(3)
    for copy in copies.values():
        copy.wait_send()


def local(picture_vectors, caption_vectors, logit_multiplier, logit_offset, partner_xor_codes):
    rows, wide = picture_vectors.shape
    in_vmem = pl.BlockSpec(memory_space=pltpu.VMEM)
    in_smem = pl.BlockSpec(memory_space=pltpu.SMEM)
    out = jax.ShapeDtypeStruct((rows, wide), F32)
    return pl.pallas_call(
        kernel,
        out_shape=(out, out),
        in_specs=[in_vmem, in_vmem, in_smem, in_smem, in_smem],
        out_specs=(in_vmem, in_vmem),
        scratch_shapes=[scratch(rows, wide)],
        compiler_params=pltpu.CompilerParams(
            collective_id=0, has_side_effects=True, vmem_limit_bytes=56 << 20
        ),
        name="contrastive_gradients",
    )(picture_vectors, caption_vectors, logit_multiplier, logit_offset, partner_xor_codes)


def solution(mesh):
    placed = (P(*WHOLE), P(*WHOLE), P(), P(), P())
    return jax.shard_map(
        local,
        mesh=mesh,
        in_specs=placed,
        out_specs=(P(*WHOLE), P(*WHOLE)),
        check_vma=False,
    )
```

```python
import jax
import jax.numpy as jnp
from jax import lax
from jax.experimental import pallas as pl
from jax.experimental.pallas import tpu as pltpu
from jax.sharding import PartitionSpec as P

EPSILON = 1e-06
MESH = pl.DeviceIdType.MESH
BF = jnp.bfloat16
F32 = jnp.float32
WHOLE = (("group", "member"), None)
PARTS = 4
OWN, LO, Y1, Y3, LO_Y1, LO_Y3, Y2, LO_Y2 = range(8)


def flip(value, code):
    if code == 0:
        return value
    if code == 1:
        return value + 1 - 2 * (value % 2)
    if code == 2:
        return (value + 2) % 4
    return 3 - value


def peer(x=0, z=0, core=0, lo=0, y=0):
    group, member = lax.axis_index("group"), lax.axis_index("member")
    at_x, at_z, at_core = group // 8, (group // 2) % 4, group % 2
    at_lo, at_y = member // 4, member % 4
    return (
        flip(at_x, x) * 8 + flip(at_z, z) * 2 + flip(at_core, core),
        flip(at_lo, lo) * 4 + flip(at_y, y),
    )


PEERS = (
    dict(core=1),
    dict(x=1),
    dict(x=3),
    dict(x=3, core=1),
    dict(z=1),
    dict(z=3),
    dict(lo=1),
    dict(y=1),
    dict(y=3),
)


def unit_rows(raw):
    values = raw.astype(F32)
    scale = lax.rsqrt(jnp.sum(values * values, axis=-1, keepdims=True) + EPSILON)
    return values * scale, scale


def back_unit(unit, scale, grad):
    return (grad - unit * jnp.sum(unit * grad, axis=-1, keepdims=True)) * scale


def choose(code, zero, one, two, three):
    low = jnp.where(code == 1, one, zero)
    high = jnp.where(code == 3, three, two)
    return jnp.where(code >= 2, high, low)


def scratch(rows, wide):
    piece = rows // PARTS
    half = piece // 2
    unit = pltpu.VMEM((rows, wide), BF)
    both = pltpu.VMEM((2 * half, wide), BF)
    pair = pltpu.VMEM((2 * piece, wide), BF)
    each = lambda ref: [ref] * PARTS
    return dict(
        img=pltpu.VMEM((8 * rows, wide), BF),
        txt=pltpu.VMEM((5 * rows, wide), BF),
        wgt=pltpu.VMEM((5 * rows, 8 * rows), BF),
        bank=each(pltpu.VMEM((8, piece, wide), BF)),
        g_near=each(both),
        g_far=each(both),
        g_s3=each(both),
        g_s21=each(both),
        g_s23=each(both),
        g_r11=each(both),
        g_r13=each(both),
        g_r21=each(both),
        g_r23=each(both),
        d_own=each(pair),
        d_core=each(pair),
        b_near=each(both),
        b_far=each(both),
        b_s3=each(both),
        b_s21=each(both),
        b_s23=each(both),
        b_r11=each(both),
        b_r13=each(both),
        b_r21=each(both),
        b_r23=each(both),
        d31_out=each(pltpu.VMEM((piece, wide), BF)),
        d31_in=each(pltpu.VMEM((piece, wide), BF)),
        z_sum=each(pltpu.VMEM((4, piece, wide), F32)),
        z_s=each(pltpu.VMEM((3, piece, wide), BF)),
        z_r2=each(pltpu.VMEM((piece, wide), BF)),
        z_r1=each(pltpu.VMEM((piece, wide), BF)),
        z_r3=each(pltpu.VMEM((piece, wide), BF)),
        d_text=pltpu.VMEM((2 * rows, wide), F32),
        d_text_in=pltpu.VMEM((rows, wide), F32),
        d_img=pltpu.VMEM((8 * rows, wide), F32),
        i_s=[unit] * 7,
        i_r=[unit] * 7,
        scale_u=pltpu.VMEM((rows, 1), F32),
        scale_v=pltpu.VMEM((rows, 1), F32),
        send=pltpu.SemaphoreType.DMA((160,)),
        recv=pltpu.SemaphoreType.DMA((160,)),
    )


def kernel(pic_ref, cap_ref, mult_ref, off_ref, code_ref, gi_ref, gt_ref, s):
    rows, wide = pic_ref.shape
    piece = rows // PARTS
    half = piece // 2
    img, txt, wgt = s["img"], s["txt"], s["wgt"]
    copies, text_seen = {}, []

    def send(name, src, dst, **to):
        at = len(copies)
        copy = pltpu.make_async_remote_copy(
            src_ref=src,
            dst_ref=dst,
            send_sem=s["send"].at[at],
            recv_sem=s["recv"].at[at],
            device_id=peer(**to),
            device_id_type=MESH,
        )
        copies[name] = copy
        copy.start()

    def arrived(*names):
        for name in names:
            copies[name].wait_recv()

    def slot(at):
        return pl.ds(at * rows, rows)

    def part(j):
        return pl.ds(j * piece, piece)

    def text_at(j):
        return 2 * rows + 3 * j * piece

    barrier = pltpu.get_barrier_semaphore()
    for to in PEERS:
        pl.semaphore_signal(barrier, inc=1, device_id=peer(**to), device_id_type=MESH)

    mult, off = mult_ref[0], off_ref[0]
    codes = [code_ref[i] for i in range(4)]
    code_a, code_b = jnp.int32(99), jnp.int32(-1)
    for code in codes:
        code_a = jnp.minimum(code_a, jnp.where(code == 1, 99, code))
        code_b = jnp.maximum(code_b, jnp.where(code == 31, -1, code))
    core_of = [code_a & 1, code_b & 1]
    z_of = [(code_a >> 1) & 3, (code_b >> 1) & 3]
    x_of = [(code_a >> 3) & 3, (code_b >> 3) & 3]

    unit_v, scale_v = unit_rows(cap_ref[...])
    s["scale_v"][...] = scale_v
    own_text = unit_v.astype(BF)
    txt[slot(0), :] = own_text
    for j in range(PARTS):
        s["bank"][j][0] = own_text[j * piece : (j + 1) * piece]
    unit_u, scale_u = unit_rows(pic_ref[...])
    s["scale_u"][...] = scale_u
    img[slot(OWN), :] = unit_u.astype(BF)
    pl.semaphore_wait(barrier, len(PEERS))

    def z_first(j):
        src = s["bank"][j].at[0]
        send(f"z1_{j}", src, s["bank"][j].at[1], z=1)
        send(f"z3_{j}", src, s["bank"][j].at[3], z=3)

    def z_second(j):
        bank = s["bank"][j]
        near, far = pl.ds(0, half), pl.ds(half, half)
        arrived(f"z1_{j}")
        send(f"z2a_{j}", bank.at[1, near], bank.at[2, near], z=3)
        arrived(f"z3_{j}")
        send(f"z2b_{j}", bank.at[3, far], bank.at[2, far], z=1)
        send(f"c1_{j}", bank.at[1], bank.at[5], core=1)
        send(f"c3_{j}", bank.at[3], bank.at[7], core=1)

    def fetch_31(j):
        bank = s["bank"][j]
        send(f"t31_{j}", bank.at[3], txt.at[pl.ds(text_at(j), piece)], x=3, core=1)

    def z_done(j):
        bank = s["bank"][j]
        arrived(f"z2a_{j}", f"z2b_{j}")
        send(f"c2_{j}", bank.at[2], bank.at[6], core=1)

    def x_send(tag, j, far, where):
        near_ref, far_ref, s3 = s[tag + "near"][j], s[tag + "far"][j], s[tag + "s3"][j]
        send(f"{tag}11_{j}", near_ref, s[tag + "r11"][j], x=1)
        for m in range(2):
            at = pl.ds(m * half, half)
            s3[at, :] = jnp.where(x_of[m] == 2, far_ref[at, :], near_ref[at, :])
        send(f"{tag}13_{j}", s3, s[tag + "r13"][j], x=3)

    def x_second(tag, j):
        far_ref = s[tag + "far"][j]
        for side, name in ((3, "11"), (1, "13")):
            arrived(f"{tag}{name}_{j}")
            got, out = s[f"{tag}r{name}"][j], s[f"{tag}s2{side}"][j]
            for m in range(2):
                at = pl.ds(m * half, half)
                out[at, :] = jnp.where(x_of[m] == 2, got[at, :], far_ref[at, :])
            send(f"{tag}2{side}_{j}", out, s[f"{tag}r2{side}"][j], x=side)

    def x_done(tag, j, m):
        at = pl.ds(m * half, half)
        r11, r13, r21, r23 = (s[f"{tag}r{n}"][j][at, :] for n in ("11", "13", "21", "23"))
        near = choose(x_of[m], s[tag + "near"][j][at, :], r11, r23, r13)
        far = choose(x_of[m], s[tag + "far"][j][at, :], r21, r21, r23)
        return near, far

    def x_text(j):
        bank = s["bank"][j]
        arrived(f"c1_{j}", f"c2_{j}", f"c3_{j}")
        for m in range(2):
            at = pl.ds(m * half, half)
            picked = bank[core_of[m] * 4 + z_of[m]]
            s["g_near"][j][at, :] = picked[:half]
            s["g_far"][j][at, :] = picked[half:]
        x_send("g_", j, None, None)

    def text_in(j):
        arrived(f"g_21_{j}", f"g_23_{j}")
        for m in range(2):
            near, far = x_done("g_", j, m)
            base = text_at(j) + (1 + m) * piece
            txt[pl.ds(base, half), :] = near
            txt[pl.ds(base + half, half), :] = far

    def weigh(start, count, at, wide_by, positive=False):
        cols = pl.ds(at * rows, wide_by * rows)
        logits = lax.dot_general(
            txt[pl.ds(start, count), :],
            img[cols, :],
            (((1,), (1,)), ((), ())),
            preferred_element_type=F32,
        )
        factor = jax.nn.sigmoid(mult * logits + off)
        if positive:
            row = lax.broadcasted_iota(jnp.int32, factor.shape, 0)
            col = lax.broadcasted_iota(jnp.int32, factor.shape, 1)
            factor = factor - jnp.where((row == col) & (row < rows), 1.0, 0.0)
        wgt[pl.ds(start, count), cols] = (mult * factor).astype(BF)

    def text_grad(start, count):
        return jnp.dot(wgt[pl.ds(start, count), :], img[...], preferred_element_type=F32)

    def image_grad(start, count, at):
        cols = pl.ds(at * rows, 2 * rows)
        return lax.dot_general(
            wgt[pl.ds(start, count), cols],
            txt[pl.ds(start, count), :],
            (((0,), (0,)), ((), ())),
            preferred_element_type=F32,
        )

    def weigh_in(j):
        arrived(f"t31_{j}")
        weigh(text_at(j), 3 * piece, 0, 8)

    def grads_out(j):
        grad = text_grad(text_at(j), 3 * piece).astype(BF)
        s["d_own"][j][...] = grad[piece:]
        send(f"dc_{j}", s["d_own"][j], s["d_core"][j], core=1)
        s["d31_out"][j][...] = grad[:piece]

    def send_31(j):
        send(f"d31_{j}", s["d31_out"][j], s["d31_in"][j], x=3, core=1)

    def grads_x(j):
        arrived(f"dc_{j}")
        own, other = s["d_own"][j], s["d_core"][j]
        for m in range(2):
            at = pl.ds(m * half, half)
            for name, base in (("near", m * piece), ("far", m * piece + half)):
                take = pl.ds(base, half)
                s["b_" + name][j][at, :] = jnp.where(core_of[m] == 1, other[take, :], own[take, :])
        x_send("b_", j, None, None)

    def grads_z(j):
        arrived(f"b_21_{j}", f"b_23_{j}", f"d31_{j}")
        total = s["z_sum"][j]
        zero = jnp.zeros((half, wide), F32)
        got = [x_done("b_", j, m) for m in range(2)]
        for h in range(2):
            at = pl.ds(h * half, half)
            a, b = got[0][h].astype(F32), got[1][h].astype(F32)
            for k in range(4):
                value = jnp.where(z_of[0] == k, a, zero) + jnp.where(z_of[1] == k, b, zero)
                if k == 3:
                    value = value + s["d31_in"][j][at, :].astype(F32)
                total[k, at, :] = value
        out = s["z_s"][j]
        out[0] = total[2].astype(BF)
        near, far = pl.ds(0, half), pl.ds(half, half)
        send(f"dz2a_{j}", out.at[0, near], s["z_r2"][j].at[near], z=3)
        send(f"dz2b_{j}", out.at[0, far], s["z_r2"][j].at[far], z=1)

    def grads_z_second(j):
        total, out, got = s["z_sum"][j], s["z_s"][j], s["z_r2"][j]
        near, far = pl.ds(0, half), pl.ds(half, half)
        arrived(f"dz2a_{j}")
        out[1, far, :] = total[1, far, :].astype(BF)
        out[1, near, :] = (total[1, near, :] + got[near, :].astype(F32)).astype(BF)
        send(f"dz1_{j}", out.at[1], s["z_r1"][j], z=1)
        arrived(f"dz2b_{j}")
        out[2, near, :] = total[3, near, :].astype(BF)
        out[2, far, :] = (total[3, far, :] + got[far, :].astype(F32)).astype(BF)
        send(f"dz3_{j}", out.at[2], s["z_r3"][j], z=3)

    def text_out(j):
        arrived(f"dz1_{j}", f"dz3_{j}")
        if not text_seen:
            text_seen.append(j)
            arrived("d1")
        total = s["z_sum"][j][0] + s["z_r1"][j][...].astype(F32) + s["z_r3"][j][...].astype(F32)
        total = total + s["d_text"][part(j), :] + s["d_text_in"][part(j), :]
        scale = s["scale_v"][part(j), :]
        unit = cap_ref[part(j), :].astype(F32) * scale
        gt_ref[part(j), :] = back_unit(unit, scale, total)

    def early(at):
        weigh(0, 2 * rows, at, 2, at == OWN)
        s["d_img"][pl.ds(at * rows, 2 * rows), :] = image_grad(0, 2 * rows, at)

    def early_text():
        s["d_text"][...] = text_grad(0, 2 * rows)
        send("d1", s["d_text"].at[slot(1)], s["d_text_in"], core=1)

    def late_image(at):
        here = pl.ds(at * rows, 2 * rows)
        s["d_img"][here, :] = s["d_img"][here, :] + image_grad(2 * rows, 3 * rows, at)

    def half_send(name, n, at, adds, h, **to):
        arrived(*(f"{add}_{h}" for add, _ in adds))
        here = pl.ds(h * rows // 2, rows // 2)
        value = s["d_img"][pl.ds(at * rows + h * rows // 2, rows // 2), :]
        for _, m in adds:
            value = value + s["i_r"][m][here, :].astype(F32)
        s["i_s"][n][here, :] = value.astype(BF)
        send(f"{name}_{h}", s["i_s"][n].at[here], s["i_r"][n].at[here], **to)

    def image_first():
        late_image(Y2)
        for h in range(2):
            half_send("u7", 0, LO_Y2, [], h, y=1)
            half_send("u6", 1, Y2, [], h, y=3)

    def image_lo_y1():
        late_image(LO_Y1)
        for h in range(2):
            half_send("u4", 2, LO_Y1, [], h, y=1)

    def image_u5(h):
        half_send("u5", 4, LO_Y3, [("u7", 0)], h, y=3)

    def image_u3(h):
        half_send("u3", 3, Y3, [], h, y=3)

    def image_u2(h):
        half_send("u2", 5, Y1, [("u6", 1)], h, y=1)

    def image_ul(h):
        half_send("ul", 6, LO, [("u4", 2), ("u5", 4)], h, lo=1)

    def image_out(h):
        arrived(*(f"{name}_{h}" for name in ("u2", "u3", "ul")))
        here = pl.ds(h * rows // 2, rows // 2)
        total = s["d_img"][here, :]
        for m in (5, 3, 6):
            total = total + s["i_r"][m][here, :].astype(F32)
        scale = s["scale_u"][here, :]
        unit = pic_ref[here, :].astype(F32) * scale
        gi_ref[here, :] = back_unit(unit, scale, total)

    def pass_image(name, source, target, h, **to):
        here = pl.ds(h * rows // 2, rows // 2)
        at = lambda n: img.at[pl.ds(n * rows + h * rows // 2, rows // 2)]
        send(f"{name}_{h}", at(source), at(target), **to)

    def start():
        pass_image("l", OWN, LO, 0, lo=1)
        pass_image("l", OWN, LO, 1, lo=1)
        for h in range(2):
            pass_image("y1", OWN, Y1, h, y=1)
            pass_image("y3", OWN, Y3, h, y=3)
        send("t1", txt.at[slot(0)], txt.at[slot(1)], core=1)

    def other_core():
        arrived("t1")
        for j in range(PARTS):
            s["bank"][j][4] = txt[pl.ds(rows + j * piece, piece), :]

    def img_lo(h):
        arrived(f"l_{h}")
        pass_image("ly3", LO, LO_Y3, h, y=3)
        pass_image("ly1", LO, LO_Y1, h, y=1)

    def img_y2(h):
        arrived(f"y1_{h}")
        pass_image("y2", Y1, Y2, h, y=3)

    def img_lo_y2(h):
        arrived(f"ly3_{h}")
        pass_image("ly2", LO_Y3, LO_Y2, h, y=1)

    def early_own():
        early(OWN)

    def early_y1():
        arrived("y3_0", "y3_1")
        early(Y1)

    def early_lo():
        arrived("ly1_0", "ly1_1")
        early(LO_Y1)

    def early_y2():
        arrived("y2_0", "y2_1", "ly2_0", "ly2_1")
        early(Y2)

    steps = [
        start,
        (z_first, 0),
        other_core,
        (img_y2, 0),
        (z_second, 0),
        (fetch_31, 0),
        (z_first, 2),
        (img_lo, 0),
        (img_y2, 1),
        early_y1,
        (z_first, 1),
        (z_done, 0),
        (x_text, 0),
        (img_lo_y2, 0),
        (z_second, 2),
        (img_lo, 1),
        early_own,
        (x_second, "g_", 0),
        (z_second, 1),
        (fetch_31, 1),
        (z_first, 3),
        (z_done, 2),
        (text_in, 0),
        (img_lo_y2, 1),
        early_lo,
        (x_text, 2),
        (fetch_31, 2),
        (z_done, 1),
        (x_text, 1),
        (z_second, 3),
        early_y2,
        (weigh_in, 0),
        (grads_out, 0),
        (send_31, 0),
        (x_second, "g_", 2),
        early_text,
        (z_done, 3),
        (x_second, "g_", 1),
        (grads_x, 0),
        (x_text, 3),
        (text_in, 2),
        (weigh_in, 2),
        (grads_out, 2),
        (send_31, 2),
        (text_in, 1),
        (weigh_in, 1),
        (grads_out, 1),
        (x_second, "b_", 0),
        (grads_x, 2),
        (grads_x, 1),
        (x_second, "g_", 3),
        (fetch_31, 3),
        (grads_z, 0),
        (x_second, "b_", 2),
        (grads_z_second, 0),
        (x_second, "b_", 1),
        (text_in, 3),
        (send_31, 1),
        (weigh_in, 3),
        (grads_out, 3),
        (send_31, 3),
        image_first,
        (grads_z, 2),
        image_lo_y1,
        (late_image, OWN),
        (text_out, 0),
        (late_image, Y1),
        (grads_x, 3),
        (grads_z, 1),
        (grads_z_second, 2),
        (image_u5, 0),
        (image_u2, 0),
        (x_second, "b_", 3),
        (grads_z_second, 1),
        (image_u5, 1),
        (image_u3, 0),
        (image_u3, 1),
        (image_u2, 1),
        (grads_z, 3),
        (text_out, 2),
        (image_ul, 0),
        (text_out, 1),
        (image_ul, 1),
        (grads_z_second, 3),
        (image_out, 0),
        (text_out, 3),
        (image_out, 1),
    ]
    for step in steps:
        if isinstance(step, tuple):
            step[0](*step[1:])
        else:
            step()
    for copy in copies.values():
        copy.wait_send()


def local(picture_vectors, caption_vectors, logit_multiplier, logit_offset, partner_xor_codes):
    rows, wide = picture_vectors.shape
    in_vmem = pl.BlockSpec(memory_space=pltpu.VMEM)
    in_smem = pl.BlockSpec(memory_space=pltpu.SMEM)
    out = jax.ShapeDtypeStruct((rows, wide), F32)
    return pl.pallas_call(
        kernel,
        out_shape=(out, out),
        in_specs=[in_vmem, in_vmem, in_smem, in_smem, in_smem],
        out_specs=(in_vmem, in_vmem),
        scratch_shapes=[scratch(rows, wide)],
        compiler_params=pltpu.CompilerParams(
            collective_id=0, has_side_effects=True, vmem_limit_bytes=56 << 20
        ),
        name="contrastive_gradients",
    )(picture_vectors, caption_vectors, logit_multiplier, logit_offset, partner_xor_codes)


def solution(mesh):
    placed = (P(*WHOLE), P(*WHOLE), P(), P(), P())
    return jax.shard_map(
        local,
        mesh=mesh,
        in_specs=placed,
        out_specs=(P(*WHOLE), P(*WHOLE)),
        check_vma=False,
    )
```

```python
import jax
import jax.numpy as jnp
from jax import lax
from jax.experimental import pallas as pl
from jax.experimental.pallas import tpu as pltpu
from jax.sharding import PartitionSpec as P

EPSILON = 1e-06
MESH = pl.DeviceIdType.MESH
BF = jnp.bfloat16
F32 = jnp.float32
WHOLE = (("group", "member"), None)
PARTS = 4
OWN, LO, Y1, Y3, LO_Y1, LO_Y3, Y2, LO_Y2 = range(8)


def flip(value, code):
    if code == 0:
        return value
    if code == 1:
        return value + 1 - 2 * (value % 2)
    if code == 2:
        return (value + 2) % 4
    return 3 - value


def peer(x=0, z=0, core=0, lo=0, y=0):
    group, member = lax.axis_index("group"), lax.axis_index("member")
    at_x, at_z, at_core = group // 8, (group // 2) % 4, group % 2
    at_lo, at_y = member // 4, member % 4
    return (
        flip(at_x, x) * 8 + flip(at_z, z) * 2 + flip(at_core, core),
        flip(at_lo, lo) * 4 + flip(at_y, y),
    )


PEERS = (
    dict(core=1),
    dict(x=1),
    dict(x=3),
    dict(x=3, core=1),
    dict(z=1),
    dict(z=3),
    dict(lo=1),
    dict(y=1),
    dict(y=3),
)


def unit_rows(raw):
    values = raw.astype(F32)
    scale = lax.rsqrt(jnp.sum(values * values, axis=-1, keepdims=True) + EPSILON)
    return values * scale, scale


def back_unit(unit, scale, grad):
    return (grad - unit * jnp.sum(unit * grad, axis=-1, keepdims=True)) * scale


def choose(code, zero, one, two, three):
    low = jnp.where(code == 1, one, zero)
    high = jnp.where(code == 3, three, two)
    return jnp.where(code >= 2, high, low)


def scratch(rows, wide):
    piece = rows // PARTS
    half = piece // 2
    unit = pltpu.VMEM((rows, wide), BF)
    both = pltpu.VMEM((2 * half, wide), BF)
    pair = pltpu.VMEM((2 * piece, wide), BF)
    each = lambda ref: [ref] * PARTS
    return dict(
        img=pltpu.VMEM((8 * rows, wide), BF),
        txt=pltpu.VMEM((5 * rows, wide), BF),
        wgt=pltpu.VMEM((5 * rows, 8 * rows), BF),
        bank=each(pltpu.VMEM((8, piece, wide), BF)),
        g_near=each(both),
        g_far=each(both),
        g_s3=each(both),
        g_s21=each(both),
        g_s23=each(both),
        g_r11=each(both),
        g_r13=each(both),
        g_r21=each(both),
        g_r23=each(both),
        d_own=each(pair),
        d_core=each(pair),
        b_near=each(both),
        b_far=each(both),
        b_s3=each(both),
        b_s21=each(both),
        b_s23=each(both),
        b_r11=each(both),
        b_r13=each(both),
        b_r21=each(both),
        b_r23=each(both),
        d31_out=each(pltpu.VMEM((piece, wide), BF)),
        d31_in=each(pltpu.VMEM((piece, wide), BF)),
        z_sum=each(pltpu.VMEM((4, piece, wide), F32)),
        z_s=each(pltpu.VMEM((3, piece, wide), BF)),
        z_r2=each(pltpu.VMEM((piece, wide), BF)),
        z_r1=each(pltpu.VMEM((piece, wide), BF)),
        z_r3=each(pltpu.VMEM((piece, wide), BF)),
        d_text=pltpu.VMEM((2 * rows, wide), F32),
        d_text_in=pltpu.VMEM((rows, wide), F32),
        d_img=pltpu.VMEM((8 * rows, wide), F32),
        i_s=[unit] * 7,
        i_r=[unit] * 7,
        pic=unit,
        cap=unit,
        mult=pltpu.SMEM((1,), F32),
        off=pltpu.SMEM((1,), F32),
        code=pltpu.SMEM((4,), jnp.int32),
        load=pltpu.SemaphoreType.DMA((5,)),
        scale_u=pltpu.VMEM((rows, 1), F32),
        scale_v=pltpu.VMEM((rows, 1), F32),
        send=pltpu.SemaphoreType.DMA((160,)),
        recv=pltpu.SemaphoreType.DMA((160,)),
    )


def kernel(pic_any, cap_any, mult_any, off_any, code_any, gi_ref, gt_ref, s):
    rows, wide = pic_any.shape
    pic_ref, cap_ref = s["pic"], s["cap"]
    mult_ref, off_ref, code_ref = s["mult"], s["off"], s["code"]
    piece = rows // PARTS
    half = piece // 2
    img, txt, wgt = s["img"], s["txt"], s["wgt"]
    copies, text_seen = {}, []

    def send(name, src, dst, **to):
        at = len(copies)
        copy = pltpu.make_async_remote_copy(
            src_ref=src,
            dst_ref=dst,
            send_sem=s["send"].at[at],
            recv_sem=s["recv"].at[at],
            device_id=peer(**to),
            device_id_type=MESH,
        )
        copies[name] = copy
        copy.start()

    def arrived(*names):
        for name in names:
            copies[name].wait_recv()

    def slot(at):
        return pl.ds(at * rows, rows)

    def part(j):
        return pl.ds(j * piece, piece)

    def text_at(j):
        return 2 * rows + 3 * j * piece

    barrier = pltpu.get_barrier_semaphore()
    for to in PEERS:
        pl.semaphore_signal(barrier, inc=1, device_id=peer(**to), device_id_type=MESH)

    loads = [
        pltpu.make_async_copy(src, dst, s["load"].at[at])
        for at, (src, dst) in enumerate(
            (
                (cap_any, cap_ref),
                (pic_any, pic_ref),
                (mult_any, mult_ref),
                (off_any, off_ref),
                (code_any, code_ref),
            )
        )
    ]
    for load in loads:
        load.start()
    loads[0].wait()
    unit_v, scale_v = unit_rows(cap_ref[...])
    s["scale_v"][...] = scale_v
    own_text = unit_v.astype(BF)
    txt[slot(0), :] = own_text
    for j in range(PARTS):
        s["bank"][j][0] = own_text[j * piece : (j + 1) * piece]
    loads[1].wait()
    unit_u, scale_u = unit_rows(pic_ref[...])
    s["scale_u"][...] = scale_u
    img[slot(OWN), :] = unit_u.astype(BF)
    for load in loads[2:]:
        load.wait()
    mult, off = mult_ref[0], off_ref[0]
    codes = [code_ref[i] for i in range(4)]
    code_a, code_b = jnp.int32(99), jnp.int32(-1)
    for code in codes:
        code_a = jnp.minimum(code_a, jnp.where(code == 1, 99, code))
        code_b = jnp.maximum(code_b, jnp.where(code == 31, -1, code))
    core_of = [code_a & 1, code_b & 1]
    z_of = [(code_a >> 1) & 3, (code_b >> 1) & 3]
    x_of = [(code_a >> 3) & 3, (code_b >> 3) & 3]
    pl.semaphore_wait(barrier, len(PEERS))

    def z_first(j):
        src = s["bank"][j].at[0]
        send(f"z1_{j}", src, s["bank"][j].at[1], z=1)
        send(f"z3_{j}", src, s["bank"][j].at[3], z=3)

    def z_second(j):
        bank = s["bank"][j]
        near, far = pl.ds(0, half), pl.ds(half, half)
        arrived(f"z1_{j}")
        send(f"z2a_{j}", bank.at[1, near], bank.at[2, near], z=3)
        arrived(f"z3_{j}")
        send(f"z2b_{j}", bank.at[3, far], bank.at[2, far], z=1)
        send(f"c1_{j}", bank.at[1], bank.at[5], core=1)
        send(f"c3_{j}", bank.at[3], bank.at[7], core=1)

    def fetch_31(j):
        bank = s["bank"][j]
        send(f"t31_{j}", bank.at[3], txt.at[pl.ds(text_at(j), piece)], x=3, core=1)

    def z_done(j):
        bank = s["bank"][j]
        arrived(f"z2a_{j}", f"z2b_{j}")
        send(f"c2_{j}", bank.at[2], bank.at[6], core=1)

    def x_send(tag, j, far, where):
        near_ref, far_ref, s3 = s[tag + "near"][j], s[tag + "far"][j], s[tag + "s3"][j]
        send(f"{tag}11_{j}", near_ref, s[tag + "r11"][j], x=1)
        for m in range(2):
            at = pl.ds(m * half, half)
            s3[at, :] = jnp.where(x_of[m] == 2, far_ref[at, :], near_ref[at, :])
        send(f"{tag}13_{j}", s3, s[tag + "r13"][j], x=3)

    def x_second(tag, j):
        far_ref = s[tag + "far"][j]
        for side, name in ((3, "11"), (1, "13")):
            arrived(f"{tag}{name}_{j}")
            got, out = s[f"{tag}r{name}"][j], s[f"{tag}s2{side}"][j]
            for m in range(2):
                at = pl.ds(m * half, half)
                out[at, :] = jnp.where(x_of[m] == 2, got[at, :], far_ref[at, :])
            send(f"{tag}2{side}_{j}", out, s[f"{tag}r2{side}"][j], x=side)

    def x_done(tag, j, m):
        at = pl.ds(m * half, half)
        r11, r13, r21, r23 = (s[f"{tag}r{n}"][j][at, :] for n in ("11", "13", "21", "23"))
        near = choose(x_of[m], s[tag + "near"][j][at, :], r11, r23, r13)
        far = choose(x_of[m], s[tag + "far"][j][at, :], r21, r21, r23)
        return near, far

    def x_text(j):
        bank = s["bank"][j]
        arrived(f"c1_{j}", f"c2_{j}", f"c3_{j}")
        for m in range(2):
            at = pl.ds(m * half, half)
            picked = bank[core_of[m] * 4 + z_of[m]]
            s["g_near"][j][at, :] = picked[:half]
            s["g_far"][j][at, :] = picked[half:]
        x_send("g_", j, None, None)

    def text_in(j):
        arrived(f"g_21_{j}", f"g_23_{j}")
        for m in range(2):
            near, far = x_done("g_", j, m)
            base = text_at(j) + (1 + m) * piece
            txt[pl.ds(base, half), :] = near
            txt[pl.ds(base + half, half), :] = far

    def weigh(start, count, at, wide_by, positive=False):
        cols = pl.ds(at * rows, wide_by * rows)
        logits = lax.dot_general(
            txt[pl.ds(start, count), :],
            img[cols, :],
            (((1,), (1,)), ((), ())),
            preferred_element_type=F32,
        )
        factor = jax.nn.sigmoid(mult * logits + off)
        if positive:
            row = lax.broadcasted_iota(jnp.int32, factor.shape, 0)
            col = lax.broadcasted_iota(jnp.int32, factor.shape, 1)
            factor = factor - jnp.where((row == col) & (row < rows), 1.0, 0.0)
        wgt[pl.ds(start, count), cols] = (mult * factor).astype(BF)

    def text_grad(start, count):
        return jnp.dot(wgt[pl.ds(start, count), :], img[...], preferred_element_type=F32)

    def image_grad(start, count, at):
        cols = pl.ds(at * rows, 2 * rows)
        return lax.dot_general(
            wgt[pl.ds(start, count), cols],
            txt[pl.ds(start, count), :],
            (((0,), (0,)), ((), ())),
            preferred_element_type=F32,
        )

    def weigh_in(j):
        arrived(f"t31_{j}")
        weigh(text_at(j), 3 * piece, 0, 8)

    def grads_out(j):
        grad = text_grad(text_at(j), 3 * piece).astype(BF)
        s["d_own"][j][...] = grad[piece:]
        send(f"dc_{j}", s["d_own"][j], s["d_core"][j], core=1)
        s["d31_out"][j][...] = grad[:piece]

    def send_31(j):
        send(f"d31_{j}", s["d31_out"][j], s["d31_in"][j], x=3, core=1)

    def grads_x(j):
        arrived(f"dc_{j}")
        own, other = s["d_own"][j], s["d_core"][j]
        for m in range(2):
            at = pl.ds(m * half, half)
            for name, base in (("near", m * piece), ("far", m * piece + half)):
                take = pl.ds(base, half)
                s["b_" + name][j][at, :] = jnp.where(core_of[m] == 1, other[take, :], own[take, :])
        x_send("b_", j, None, None)

    def grads_z(j):
        arrived(f"b_21_{j}", f"b_23_{j}", f"d31_{j}")
        total = s["z_sum"][j]
        zero = jnp.zeros((half, wide), F32)
        got = [x_done("b_", j, m) for m in range(2)]
        for h in range(2):
            at = pl.ds(h * half, half)
            a, b = got[0][h].astype(F32), got[1][h].astype(F32)
            for k in range(4):
                value = jnp.where(z_of[0] == k, a, zero) + jnp.where(z_of[1] == k, b, zero)
                if k == 3:
                    value = value + s["d31_in"][j][at, :].astype(F32)
                total[k, at, :] = value
        out = s["z_s"][j]
        out[0] = total[2].astype(BF)
        near, far = pl.ds(0, half), pl.ds(half, half)
        send(f"dz2a_{j}", out.at[0, near], s["z_r2"][j].at[near], z=3)
        send(f"dz2b_{j}", out.at[0, far], s["z_r2"][j].at[far], z=1)

    def grads_z_second(j):
        total, out, got = s["z_sum"][j], s["z_s"][j], s["z_r2"][j]
        near, far = pl.ds(0, half), pl.ds(half, half)
        arrived(f"dz2a_{j}")
        out[1, far, :] = total[1, far, :].astype(BF)
        out[1, near, :] = (total[1, near, :] + got[near, :].astype(F32)).astype(BF)
        send(f"dz1_{j}", out.at[1], s["z_r1"][j], z=1)
        arrived(f"dz2b_{j}")
        out[2, near, :] = total[3, near, :].astype(BF)
        out[2, far, :] = (total[3, far, :] + got[far, :].astype(F32)).astype(BF)
        send(f"dz3_{j}", out.at[2], s["z_r3"][j], z=3)

    def text_out(j):
        arrived(f"dz1_{j}", f"dz3_{j}")
        if not text_seen:
            text_seen.append(j)
            arrived("d1")
        total = s["z_sum"][j][0] + s["z_r1"][j][...].astype(F32) + s["z_r3"][j][...].astype(F32)
        total = total + s["d_text"][part(j), :] + s["d_text_in"][part(j), :]
        scale = s["scale_v"][part(j), :]
        unit = cap_ref[part(j), :].astype(F32) * scale
        gt_ref[part(j), :] = back_unit(unit, scale, total)

    def early(at):
        weigh(0, 2 * rows, at, 2, at == OWN)
        s["d_img"][pl.ds(at * rows, 2 * rows), :] = image_grad(0, 2 * rows, at)

    def early_text():
        s["d_text"][...] = text_grad(0, 2 * rows)
        send("d1", s["d_text"].at[slot(1)], s["d_text_in"], core=1)

    def late_image(at):
        here = pl.ds(at * rows, 2 * rows)
        s["d_img"][here, :] = s["d_img"][here, :] + image_grad(2 * rows, 3 * rows, at)

    def half_send(name, n, at, adds, h, **to):
        arrived(*(f"{add}_{h}" for add, _ in adds))
        here = pl.ds(h * rows // 2, rows // 2)
        value = s["d_img"][pl.ds(at * rows + h * rows // 2, rows // 2), :]
        for _, m in adds:
            value = value + s["i_r"][m][here, :].astype(F32)
        s["i_s"][n][here, :] = value.astype(BF)
        send(f"{name}_{h}", s["i_s"][n].at[here], s["i_r"][n].at[here], **to)

    def image_first():
        late_image(Y2)
        for h in range(2):
            half_send("u7", 0, LO_Y2, [], h, y=1)
            half_send("u6", 1, Y2, [], h, y=3)

    def image_lo_y1():
        late_image(LO_Y1)
        for h in range(2):
            half_send("u4", 2, LO_Y1, [], h, y=1)

    def image_u5(h):
        half_send("u5", 4, LO_Y3, [("u7", 0)], h, y=3)

    def image_u3(h):
        half_send("u3", 3, Y3, [], h, y=3)

    def image_u2(h):
        half_send("u2", 5, Y1, [("u6", 1)], h, y=1)

    def image_ul(h):
        half_send("ul", 6, LO, [("u4", 2), ("u5", 4)], h, lo=1)

    def image_out(h):
        arrived(*(f"{name}_{h}" for name in ("u2", "u3", "ul")))
        here = pl.ds(h * rows // 2, rows // 2)
        total = s["d_img"][here, :]
        for m in (5, 3, 6):
            total = total + s["i_r"][m][here, :].astype(F32)
        scale = s["scale_u"][here, :]
        unit = pic_ref[here, :].astype(F32) * scale
        gi_ref[here, :] = back_unit(unit, scale, total)

    def pass_image(name, source, target, h, **to):
        here = pl.ds(h * rows // 2, rows // 2)
        at = lambda n: img.at[pl.ds(n * rows + h * rows // 2, rows // 2)]
        send(f"{name}_{h}", at(source), at(target), **to)

    def start_lo(h):
        pass_image("l", OWN, LO, h, lo=1)

    def start():
        for h in range(2):
            pass_image("y1", OWN, Y1, h, y=1)
            pass_image("y3", OWN, Y3, h, y=3)
        send("t1", txt.at[slot(0)], txt.at[slot(1)], core=1)

    def other_core():
        arrived("t1")
        for j in range(PARTS):
            s["bank"][j][4] = txt[pl.ds(rows + j * piece, piece), :]

    def img_lo(h):
        arrived(f"l_{h}")
        pass_image("ly3", LO, LO_Y3, h, y=3)
        pass_image("ly1", LO, LO_Y1, h, y=1)

    def img_y2(h):
        arrived(f"y1_{h}")
        pass_image("y2", Y1, Y2, h, y=3)

    def img_lo_y2(h):
        arrived(f"ly3_{h}")
        pass_image("ly2", LO_Y3, LO_Y2, h, y=1)

    def early_own():
        early(OWN)

    def early_y1():
        arrived("y3_0", "y3_1")
        early(Y1)

    def early_lo():
        arrived("ly1_0", "ly1_1")
        early(LO_Y1)

    def early_y2():
        arrived("y2_0", "y2_1", "ly2_0", "ly2_1")
        early(Y2)

    steps = [
        start,
        (start_lo, 0),
        (z_first, 0),
        (img_y2, 0),
        (start_lo, 1),
        other_core,
        (z_second, 0),
        (img_lo, 0),
        (z_done, 0),
        (z_first, 2),
        (x_text, 0),
        (img_lo, 1),
        (fetch_31, 0),
        (img_y2, 1),
        (z_first, 1),
        early_y1,
        (z_second, 2),
        (x_second, "g_", 0),
        (img_lo_y2, 1),
        (img_lo_y2, 0),
        (z_second, 1),
        (z_done, 2),
        (z_first, 3),
        (fetch_31, 1),
        (x_text, 2),
        early_lo,
        (z_done, 1),
        early_own,
        (fetch_31, 2),
        (text_in, 0),
        (x_text, 1),
        early_y2,
        (x_second, "g_", 2),
        (weigh_in, 0),
        (grads_out, 0),
        (z_second, 3),
        (send_31, 0),
        (x_second, "g_", 1),
        (z_done, 3),
        (grads_x, 0),
        (text_in, 2),
        (x_text, 3),
        (weigh_in, 2),
        (text_in, 1),
        (grads_out, 2),
        (fetch_31, 3),
        (weigh_in, 1),
        (x_second, "b_", 0),
        (grads_x, 2),
        (grads_out, 1),
        early_text,
        (x_second, "g_", 3),
        (grads_x, 1),
        (x_second, "b_", 2),
        (grads_z, 0),
        (send_31, 2),
        (text_in, 3),
        (weigh_in, 3),
        (send_31, 1),
        image_first,
        (grads_out, 3),
        (grads_z_second, 0),
        (x_second, "b_", 1),
        (grads_x, 3),
        image_lo_y1,
        (grads_z, 2),
        (grads_z, 1),
        (image_u5, 0),
        (grads_z_second, 2),
        (image_u5, 1),
        (send_31, 3),
        (late_image, Y1),
        (x_second, "b_", 3),
        (late_image, OWN),
        (grads_z_second, 1),
        (image_u2, 0),
        (image_u3, 0),
        (grads_z, 3),
        (image_u3, 1),
        (image_u2, 1),
        (image_ul, 0),
        (text_out, 0),
        (grads_z_second, 3),
        (image_out, 0),
        (image_ul, 1),
        (text_out, 1),
        (text_out, 2),
        (text_out, 3),
        (image_out, 1),
    ]
    for step in steps:
        if isinstance(step, tuple):
            step[0](*step[1:])
        else:
            step()
    for copy in copies.values():
        copy.wait_send()


def local(picture_vectors, caption_vectors, logit_multiplier, logit_offset, partner_xor_codes):
    rows, wide = picture_vectors.shape
    in_vmem = pl.BlockSpec(memory_space=pltpu.VMEM)
    anywhere = pl.BlockSpec(memory_space=pl.ANY)
    out = jax.ShapeDtypeStruct((rows, wide), F32)
    return pl.pallas_call(
        kernel,
        out_shape=(out, out),
        in_specs=[anywhere] * 5,
        out_specs=(in_vmem, in_vmem),
        scratch_shapes=[scratch(rows, wide)],
        compiler_params=pltpu.CompilerParams(
            collective_id=0, has_side_effects=True, vmem_limit_bytes=38 << 20
        ),
        name="contrastive_gradients",
    )(picture_vectors, caption_vectors, logit_multiplier, logit_offset, partner_xor_codes)


def solution(mesh):
    placed = (P(*WHOLE), P(*WHOLE), P(), P(), P())
    return jax.shard_map(
        local,
        mesh=mesh,
        in_specs=placed,
        out_specs=(P(*WHOLE), P(*WHOLE)),
        check_vma=False,
    )
```

```python
import functools

import jax
import jax.numpy as jnp
from jax import lax
from jax.experimental import pallas as pl
from jax.experimental.pallas import tpu as pltpu
from jax.sharding import PartitionSpec as P

EPSILON = 1e-06
MESH = pl.DeviceIdType.MESH
BF = jnp.bfloat16
F32 = jnp.float32
WHOLE = (("group", "member"), None)
PARTS = 4
OWN, LO, Y1, Y3, LO_Y1, LO_Y3, Y2, LO_Y2 = range(8)


def flip(value, code):
    if code == 0:
        return value
    if code == 1:
        return value + 1 - 2 * (value % 2)
    if code == 2:
        return (value + 2) % 4
    return 3 - value


def peer(x=0, z=0, core=0, lo=0, y=0):
    group, member = lax.axis_index("group"), lax.axis_index("member")
    at_x, at_z, at_core = group // 8, (group // 2) % 4, group % 2
    at_lo, at_y = member // 4, member % 4
    return (
        flip(at_x, x) * 8 + flip(at_z, z) * 2 + flip(at_core, core),
        flip(at_lo, lo) * 4 + flip(at_y, y),
    )


PEERS = (
    dict(core=1),
    dict(x=1),
    dict(x=3),
    dict(x=3, core=1),
    dict(z=1),
    dict(z=3),
    dict(lo=1),
    dict(y=1),
    dict(y=3),
)


def unit_rows(raw):
    values = raw.astype(F32)
    scale = lax.rsqrt(jnp.sum(values * values, axis=-1, keepdims=True) + EPSILON)
    return values * scale, scale


def back_unit(unit, scale, grad):
    return (grad - unit * jnp.sum(unit * grad, axis=-1, keepdims=True)) * scale


def choose(code, zero, one, two, three):
    low = jnp.where(code == 1, one, zero)
    high = jnp.where(code == 3, three, two)
    return jnp.where(code >= 2, high, low)


def scratch(rows, wide):
    piece = rows // PARTS
    half = piece // 2
    unit = pltpu.VMEM((rows, wide), BF)
    both = pltpu.VMEM((2 * half, wide), BF)
    pair = pltpu.VMEM((2 * piece, wide), BF)
    each = lambda ref: [ref] * PARTS
    return dict(
        img=pltpu.VMEM((8 * rows, wide), BF),
        txt=pltpu.VMEM((5 * rows, wide), BF),
        wgt=pltpu.VMEM((5 * rows, 8 * rows), BF),
        bank=each(pltpu.VMEM((8, piece, wide), BF)),
        g_near=each(both),
        g_far=each(both),
        g_s3=each(both),
        g_s21=each(both),
        g_s23=each(both),
        g_r11=each(both),
        g_r13=each(both),
        g_r21=each(both),
        g_r23=each(both),
        d_own=each(pair),
        d_core=each(pair),
        b_near=each(both),
        b_far=each(both),
        b_s3=each(both),
        b_s21=each(both),
        b_s23=each(both),
        b_r11=each(both),
        b_r13=each(both),
        b_r21=each(both),
        b_r23=each(both),
        d31_out=each(pltpu.VMEM((piece, wide), BF)),
        d31_in=each(pltpu.VMEM((piece, wide), BF)),
        z_sum=each(pltpu.VMEM((4, piece, wide), F32)),
        z_s=each(pltpu.VMEM((3, piece, wide), BF)),
        z_out=each(pltpu.VMEM((piece, wide), BF)),
        z_r2=each(pltpu.VMEM((piece, wide), BF)),
        z_r1=each(pltpu.VMEM((piece, wide), BF)),
        z_r3=each(pltpu.VMEM((piece, wide), BF)),
        d_text=pltpu.VMEM((2 * rows, wide), F32),
        d_text_in=pltpu.VMEM((rows, wide), F32),
        d_img=pltpu.VMEM((8 * rows, wide), F32),
        i_s=[unit] * 7,
        i_r=[unit] * 7,
        pic=unit,
        cap=unit,
        mult=pltpu.SMEM((1,), F32),
        off=pltpu.SMEM((1,), F32),
        code=pltpu.SMEM((4,), jnp.int32),
        load=pltpu.SemaphoreType.DMA((5,)),
        scale_u=pltpu.VMEM((rows, 1), F32),
        scale_v=pltpu.VMEM((rows, 1), F32),
        send=pltpu.SemaphoreType.DMA((160,)),
        recv=pltpu.SemaphoreType.DMA((160,)),
    )


def kernel(lite, pic_any, cap_any, mult_any, off_any, code_any, gi_ref, gt_ref, s):
    rows, wide = pic_any.shape
    pic_ref, cap_ref = s["pic"], s["cap"]
    mult_ref, off_ref, code_ref = s["mult"], s["off"], s["code"]
    piece = rows // PARTS
    half = piece // 2
    img, txt, wgt = s["img"], s["txt"], s["wgt"]
    copies, text_seen = {}, []

    def send(name, src, dst, **to):
        at = len(copies)
        copy = pltpu.make_async_remote_copy(
            src_ref=src,
            dst_ref=dst,
            send_sem=s["send"].at[at],
            recv_sem=s["recv"].at[at],
            device_id=peer(**to),
            device_id_type=MESH,
        )
        copies[name] = copy
        copy.start()

    def arrived(*names):
        for name in names:
            copies[name].wait_recv()

    def slot(at):
        return pl.ds(at * rows, rows)

    def part(j):
        return pl.ds(j * piece, piece)

    def text_at(j):
        return 2 * rows + 3 * j * piece

    barrier = pltpu.get_barrier_semaphore()
    for to in PEERS:
        pl.semaphore_signal(barrier, inc=1, device_id=peer(**to), device_id_type=MESH)

    loads = [
        pltpu.make_async_copy(src, dst, s["load"].at[at])
        for at, (src, dst) in enumerate(
            (
                (cap_any, cap_ref),
                (pic_any, pic_ref),
                (mult_any, mult_ref),
                (off_any, off_ref),
                (code_any, code_ref),
            )
        )
    ]
    for load in loads:
        load.start()
    loads[0].wait()
    unit_v, scale_v = unit_rows(cap_ref[...])
    s["scale_v"][...] = scale_v
    own_text = unit_v.astype(BF)
    txt[slot(0), :] = own_text
    for j in range(PARTS):
        s["bank"][j][0] = own_text[j * piece : (j + 1) * piece]
    loads[1].wait()
    unit_u, scale_u = unit_rows(pic_ref[...])
    s["scale_u"][...] = scale_u
    img[slot(OWN), :] = unit_u.astype(BF)
    for load in loads[2:]:
        load.wait()
    mult, off = mult_ref[0], off_ref[0]
    codes = [code_ref[i] for i in range(4)]
    code_a, code_b = jnp.int32(99), jnp.int32(-1)
    for code in codes:
        code_a = jnp.minimum(code_a, jnp.where(code == 1, 99, code))
        code_b = jnp.maximum(code_b, jnp.where(code == 31, -1, code))
    core_of = [code_a & 1, code_b & 1]
    z_of = [(code_a >> 1) & 3, (code_b >> 1) & 3]
    x_of = [(code_a >> 3) & 3, (code_b >> 3) & 3]
    need_1 = (z_of[0] == 1) | (z_of[1] == 1)
    slot_of = [jnp.where(z == 2, 1, z) for z in z_of] if lite else z_of
    pl.semaphore_wait(barrier, len(PEERS))

    def z_first(j):
        src = s["bank"][j].at[0]
        if lite:
            send(f"z3_{j}", src, s["bank"][j].at[3], z=3)
            return
        send(f"z1_{j}", src, s["bank"][j].at[1], z=1)
        send(f"z3_{j}", src, s["bank"][j].at[3], z=3)

    def z_second(j):
        bank = s["bank"][j]
        if lite:
            arrived(f"z3_{j}")
            s["z_out"][j][...] = jnp.where(need_1, bank[0], bank[3])
            send(f"z1_{j}", s["z_out"][j], bank.at[1], z=1)
            send(f"c3_{j}", bank.at[3], bank.at[7], core=1)
            return
        near, far = pl.ds(0, half), pl.ds(half, half)
        arrived(f"z1_{j}")
        send(f"z2a_{j}", bank.at[1, near], bank.at[2, near], z=3)
        arrived(f"z3_{j}")
        send(f"z2b_{j}", bank.at[3, far], bank.at[2, far], z=1)
        send(f"c1_{j}", bank.at[1], bank.at[5], core=1)
        send(f"c3_{j}", bank.at[3], bank.at[7], core=1)

    def fetch_31(j):
        bank = s["bank"][j]
        send(f"t31_{j}", bank.at[3], txt.at[pl.ds(text_at(j), piece)], x=3, core=1)

    def z_done(j):
        bank = s["bank"][j]
        if lite:
            arrived(f"z1_{j}")
            send(f"c1_{j}", bank.at[1], bank.at[5], core=1)
            return
        arrived(f"z2a_{j}", f"z2b_{j}")
        send(f"c2_{j}", bank.at[2], bank.at[6], core=1)

    def x_send(tag, j, far, where):
        near_ref, far_ref, s3 = s[tag + "near"][j], s[tag + "far"][j], s[tag + "s3"][j]
        send(f"{tag}11_{j}", near_ref, s[tag + "r11"][j], x=1)
        for m in range(2):
            at = pl.ds(m * half, half)
            s3[at, :] = jnp.where(x_of[m] == 2, far_ref[at, :], near_ref[at, :])
        send(f"{tag}13_{j}", s3, s[tag + "r13"][j], x=3)

    def x_second(tag, j):
        far_ref = s[tag + "far"][j]
        for side, name in ((3, "11"), (1, "13")):
            arrived(f"{tag}{name}_{j}")
            got, out = s[f"{tag}r{name}"][j], s[f"{tag}s2{side}"][j]
            for m in range(2):
                at = pl.ds(m * half, half)
                out[at, :] = jnp.where(x_of[m] == 2, got[at, :], far_ref[at, :])
            send(f"{tag}2{side}_{j}", out, s[f"{tag}r2{side}"][j], x=side)

    def x_done(tag, j, m):
        at = pl.ds(m * half, half)
        r11, r13, r21, r23 = (s[f"{tag}r{n}"][j][at, :] for n in ("11", "13", "21", "23"))
        near = choose(x_of[m], s[tag + "near"][j][at, :], r11, r23, r13)
        far = choose(x_of[m], s[tag + "far"][j][at, :], r21, r21, r23)
        return near, far

    def x_text(j):
        bank = s["bank"][j]
        arrived(f"c1_{j}", f"c3_{j}")
        if not lite:
            arrived(f"c2_{j}")
        for m in range(2):
            at = pl.ds(m * half, half)
            picked = bank[core_of[m] * 4 + slot_of[m]]
            s["g_near"][j][at, :] = picked[:half]
            s["g_far"][j][at, :] = picked[half:]
        x_send("g_", j, None, None)

    def text_in(j):
        arrived(f"g_21_{j}", f"g_23_{j}")
        for m in range(2):
            near, far = x_done("g_", j, m)
            base = text_at(j) + (1 + m) * piece
            txt[pl.ds(base, half), :] = near
            txt[pl.ds(base + half, half), :] = far

    def weigh(start, count, at, wide_by, positive=False):
        cols = pl.ds(at * rows, wide_by * rows)
        logits = lax.dot_general(
            txt[pl.ds(start, count), :],
            img[cols, :],
            (((1,), (1,)), ((), ())),
            preferred_element_type=F32,
        )
        factor = jax.nn.sigmoid(mult * logits + off)
        if positive:
            row = lax.broadcasted_iota(jnp.int32, factor.shape, 0)
            col = lax.broadcasted_iota(jnp.int32, factor.shape, 1)
            factor = factor - jnp.where((row == col) & (row < rows), 1.0, 0.0)
        wgt[pl.ds(start, count), cols] = (mult * factor).astype(BF)

    def text_grad(start, count):
        return jnp.dot(wgt[pl.ds(start, count), :], img[...], preferred_element_type=F32)

    def image_grad(start, count, at):
        cols = pl.ds(at * rows, 2 * rows)
        return lax.dot_general(
            wgt[pl.ds(start, count), cols],
            txt[pl.ds(start, count), :],
            (((0,), (0,)), ((), ())),
            preferred_element_type=F32,
        )

    def weigh_in(j):
        arrived(f"t31_{j}")
        weigh(text_at(j), 3 * piece, 0, 8)

    def grads_out(j):
        grad = text_grad(text_at(j), 3 * piece).astype(BF)
        s["d_own"][j][...] = grad[piece:]
        send(f"dc_{j}", s["d_own"][j], s["d_core"][j], core=1)
        s["d31_out"][j][...] = grad[:piece]

    def send_31(j):
        send(f"d31_{j}", s["d31_out"][j], s["d31_in"][j], x=3, core=1)

    def grads_x(j):
        arrived(f"dc_{j}")
        own, other = s["d_own"][j], s["d_core"][j]
        for m in range(2):
            at = pl.ds(m * half, half)
            for name, base in (("near", m * piece), ("far", m * piece + half)):
                take = pl.ds(base, half)
                s["b_" + name][j][at, :] = jnp.where(core_of[m] == 1, other[take, :], own[take, :])
        x_send("b_", j, None, None)

    def grads_z(j):
        arrived(f"b_21_{j}", f"b_23_{j}", f"d31_{j}")
        total = s["z_sum"][j]
        zero = jnp.zeros((half, wide), F32)
        got = [x_done("b_", j, m) for m in range(2)]
        for h in range(2):
            at = pl.ds(h * half, half)
            a, b = got[0][h].astype(F32), got[1][h].astype(F32)
            for k in (0, 1, 3) if lite else range(4):
                to_k = [slot == k for slot in slot_of]
                value = jnp.where(to_k[0], a, zero) + jnp.where(to_k[1], b, zero)
                if k == 3:
                    value = value + s["d31_in"][j][at, :].astype(F32)
                total[k, at, :] = value
        out = s["z_s"][j]
        if lite:
            out[1] = total[1].astype(BF)
            send(f"dz1_{j}", out.at[1], s["z_r1"][j], z=1)
            return
        out[0] = total[2].astype(BF)
        near, far = pl.ds(0, half), pl.ds(half, half)
        send(f"dz2a_{j}", out.at[0, near], s["z_r2"][j].at[near], z=3)
        send(f"dz2b_{j}", out.at[0, far], s["z_r2"][j].at[far], z=1)

    def grads_z_second(j):
        total, out, got = s["z_sum"][j], s["z_s"][j], s["z_r2"][j]
        if lite:
            arrived(f"dz1_{j}")
            came = s["z_r1"][j][...].astype(F32)
            zero = jnp.zeros_like(came)
            out[2] = (total[3] + jnp.where(need_1, zero, came)).astype(BF)
            send(f"dz3_{j}", out.at[2], s["z_r3"][j], z=3)
            total[0] = total[0] + jnp.where(need_1, came, zero)
            return
        near, far = pl.ds(0, half), pl.ds(half, half)
        arrived(f"dz2a_{j}")
        out[1, far, :] = total[1, far, :].astype(BF)
        out[1, near, :] = (total[1, near, :] + got[near, :].astype(F32)).astype(BF)
        send(f"dz1_{j}", out.at[1], s["z_r1"][j], z=1)
        arrived(f"dz2b_{j}")
        out[2, near, :] = total[3, near, :].astype(BF)
        out[2, far, :] = (total[3, far, :] + got[far, :].astype(F32)).astype(BF)
        send(f"dz3_{j}", out.at[2], s["z_r3"][j], z=3)

    def text_out(j):
        arrived(f"dz3_{j}")
        if not text_seen:
            text_seen.append(j)
            arrived("d1")
        total = s["z_sum"][j][0] + s["z_r3"][j][...].astype(F32)
        if not lite:
            arrived(f"dz1_{j}")
            total = total + s["z_r1"][j][...].astype(F32)
        total = total + s["d_text"][part(j), :] + s["d_text_in"][part(j), :]
        scale = s["scale_v"][part(j), :]
        unit = cap_ref[part(j), :].astype(F32) * scale
        gt_ref[part(j), :] = back_unit(unit, scale, total)

    def early(at):
        weigh(0, 2 * rows, at, 2, at == OWN)
        s["d_img"][pl.ds(at * rows, 2 * rows), :] = image_grad(0, 2 * rows, at)

    def early_text():
        s["d_text"][...] = text_grad(0, 2 * rows)
        send("d1", s["d_text"].at[slot(1)], s["d_text_in"], core=1)

    def late_image(at):
        here = pl.ds(at * rows, 2 * rows)
        s["d_img"][here, :] = s["d_img"][here, :] + image_grad(2 * rows, 3 * rows, at)

    def half_send(name, n, at, adds, h, **to):
        arrived(*(f"{add}_{h}" for add, _ in adds))
        here = pl.ds(h * rows // 2, rows // 2)
        value = s["d_img"][pl.ds(at * rows + h * rows // 2, rows // 2), :]
        for _, m in adds:
            value = value + s["i_r"][m][here, :].astype(F32)
        s["i_s"][n][here, :] = value.astype(BF)
        send(f"{name}_{h}", s["i_s"][n].at[here], s["i_r"][n].at[here], **to)

    def image_first():
        late_image(Y2)
        for h in range(2):
            half_send("u7", 0, LO_Y2, [], h, y=1)
            half_send("u6", 1, Y2, [], h, y=3)

    def image_lo_y1():
        late_image(LO_Y1)
        for h in range(2):
            half_send("u4", 2, LO_Y1, [], h, y=1)

    def image_u5(h):
        half_send("u5", 4, LO_Y3, [("u7", 0)], h, y=3)

    def image_u3(h):
        half_send("u3", 3, Y3, [], h, y=3)

    def image_u2(h):
        half_send("u2", 5, Y1, [("u6", 1)], h, y=1)

    def image_ul(h):
        half_send("ul", 6, LO, [("u4", 2), ("u5", 4)], h, lo=1)

    def image_out(h):
        arrived(*(f"{name}_{h}" for name in ("u2", "u3", "ul")))
        here = pl.ds(h * rows // 2, rows // 2)
        total = s["d_img"][here, :]
        for m in (5, 3, 6):
            total = total + s["i_r"][m][here, :].astype(F32)
        scale = s["scale_u"][here, :]
        unit = pic_ref[here, :].astype(F32) * scale
        gi_ref[here, :] = back_unit(unit, scale, total)

    def pass_image(name, source, target, h, **to):
        here = pl.ds(h * rows // 2, rows // 2)
        at = lambda n: img.at[pl.ds(n * rows + h * rows // 2, rows // 2)]
        send(f"{name}_{h}", at(source), at(target), **to)

    def start_lo(h):
        pass_image("l", OWN, LO, h, lo=1)

    def start():
        for h in range(2):
            pass_image("y1", OWN, Y1, h, y=1)
            pass_image("y3", OWN, Y3, h, y=3)
        send("t1", txt.at[slot(0)], txt.at[slot(1)], core=1)

    def other_core():
        arrived("t1")
        for j in range(PARTS):
            s["bank"][j][4] = txt[pl.ds(rows + j * piece, piece), :]

    def img_lo(h):
        arrived(f"l_{h}")
        pass_image("ly3", LO, LO_Y3, h, y=3)
        pass_image("ly1", LO, LO_Y1, h, y=1)

    def img_y2(h):
        arrived(f"y1_{h}")
        pass_image("y2", Y1, Y2, h, y=3)

    def img_lo_y2(h):
        arrived(f"ly3_{h}")
        pass_image("ly2", LO_Y3, LO_Y2, h, y=1)

    def early_own():
        early(OWN)

    def early_y1():
        arrived("y3_0", "y3_1")
        early(Y1)

    def early_lo():
        arrived("ly1_0", "ly1_1")
        early(LO_Y1)

    def early_y2():
        arrived("y2_0", "y2_1", "ly2_0", "ly2_1")
        early(Y2)

    if lite:
        steps = [
            start,
            (z_first, 0),
            (z_first, 1),
            (start_lo, 0),
            other_core,
            (z_second, 0),
            (fetch_31, 0),
            (z_first, 2),
            (start_lo, 1),
            (img_lo, 0),
            (z_second, 1),
            (fetch_31, 1),
            (img_y2, 0),
            (z_done, 0),
            (x_text, 0),
            (z_second, 2),
            (img_lo_y2, 0),
            (z_done, 1),
            (z_first, 3),
            (img_lo, 1),
            (img_y2, 1),
            (x_text, 1),
            (x_second, "g_", 0),
            (z_done, 2),
            (z_second, 3),
            (x_second, "g_", 1),
            (img_lo_y2, 1),
            (x_text, 2),
            early_own,
            early_lo,
            (text_in, 0),
            (text_in, 1),
            (fetch_31, 2),
            early_y1,
            (z_done, 3),
            (x_second, "g_", 2),
            early_y2,
            (weigh_in, 0),
            (x_text, 3),
            (grads_out, 0),
            (weigh_in, 1),
            (fetch_31, 3),
            (grads_out, 1),
            (grads_x, 0),
            (send_31, 0),
            (x_second, "g_", 3),
            (text_in, 2),
            early_text,
            (weigh_in, 2),
            (grads_x, 1),
            (x_second, "b_", 0),
            (grads_out, 2),
            (text_in, 3),
            (weigh_in, 3),
            image_first,
            (send_31, 1),
            (grads_out, 3),
            (x_second, "b_", 1),
            (grads_x, 2),
            image_lo_y1,
            (grads_z, 0),
            (grads_z, 1),
            (send_31, 2),
            (x_second, "b_", 2),
            (late_image, Y1),
            (late_image, OWN),
            (grads_z_second, 0),
            (grads_x, 3),
            (image_u5, 0),
            (grads_z, 2),
            (send_31, 3),
            (grads_z_second, 1),
            (image_u2, 1),
            (x_second, "b_", 3),
            (image_u2, 0),
            (image_u5, 1),
            (image_u3, 0),
            (image_ul, 0),
            (grads_z, 3),
            (image_ul, 1),
            (text_out, 0),
            (grads_z_second, 2),
            (image_u3, 1),
            (image_out, 0),
            (text_out, 1),
            (grads_z_second, 3),
            (text_out, 2),
            (text_out, 3),
            (image_out, 1),
        ]
    else:
        steps = [
            start,
            (start_lo, 0),
            (z_first, 0),
            (img_y2, 0),
            (start_lo, 1),
            other_core,
            (z_second, 0),
            (img_lo, 0),
            (z_done, 0),
            (z_first, 2),
            (x_text, 0),
            (img_lo, 1),
            (fetch_31, 0),
            (img_y2, 1),
            (z_first, 1),
            early_y1,
            (z_second, 2),
            (x_second, "g_", 0),
            (img_lo_y2, 1),
            (img_lo_y2, 0),
            (z_second, 1),
            (z_done, 2),
            (z_first, 3),
            (fetch_31, 1),
            (x_text, 2),
            early_lo,
            (z_done, 1),
            early_own,
            (fetch_31, 2),
            (text_in, 0),
            (x_text, 1),
            early_y2,
            (x_second, "g_", 2),
            (weigh_in, 0),
            (grads_out, 0),
            (z_second, 3),
            (send_31, 0),
            (x_second, "g_", 1),
            (z_done, 3),
            (grads_x, 0),
            (text_in, 2),
            (x_text, 3),
            (weigh_in, 2),
            (text_in, 1),
            (grads_out, 2),
            (fetch_31, 3),
            (weigh_in, 1),
            (x_second, "b_", 0),
            (grads_x, 2),
            (grads_out, 1),
            early_text,
            (x_second, "g_", 3),
            (grads_x, 1),
            (x_second, "b_", 2),
            (grads_z, 0),
            (send_31, 2),
            (text_in, 3),
            (weigh_in, 3),
            (send_31, 1),
            image_first,
            (grads_out, 3),
            (grads_z_second, 0),
            (x_second, "b_", 1),
            (grads_x, 3),
            image_lo_y1,
            (grads_z, 2),
            (grads_z, 1),
            (image_u5, 0),
            (grads_z_second, 2),
            (image_u5, 1),
            (send_31, 3),
            (late_image, Y1),
            (x_second, "b_", 3),
            (late_image, OWN),
            (grads_z_second, 1),
            (image_u2, 0),
            (image_u3, 0),
            (grads_z, 3),
            (image_u3, 1),
            (image_u2, 1),
            (image_ul, 0),
            (text_out, 0),
            (grads_z_second, 3),
            (image_out, 0),
            (image_ul, 1),
            (text_out, 1),
            (text_out, 2),
            (text_out, 3),
            (image_out, 1),
        ]
    for step in steps:
        if isinstance(step, tuple):
            step[0](*step[1:])
        else:
            step()
    for copy in copies.values():
        copy.wait_send()


def call(lite, *args):
    rows, wide = args[0].shape
    in_vmem = pl.BlockSpec(memory_space=pltpu.VMEM)
    anywhere = pl.BlockSpec(memory_space=pl.ANY)
    out = jax.ShapeDtypeStruct((rows, wide), F32)
    return pl.pallas_call(
        functools.partial(kernel, lite),
        out_shape=(out, out),
        in_specs=[anywhere] * 5,
        out_specs=(in_vmem, in_vmem),
        scratch_shapes=[scratch(rows, wide)],
        compiler_params=pltpu.CompilerParams(
            collective_id=0 if lite else 1, has_side_effects=True, vmem_limit_bytes=38 << 20
        ),
        name="contrastive_lite" if lite else "contrastive_full",
    )(*args)


def local(*args):
    z_codes = (args[4] >> 1) & 3
    both = jnp.any(z_codes == 1) & jnp.any(z_codes == 2)
    return lax.cond(both, functools.partial(call, False), functools.partial(call, True), *args)


def solution(mesh):
    placed = (P(*WHOLE), P(*WHOLE), P(), P(), P())
    return jax.shard_map(
        local,
        mesh=mesh,
        in_specs=placed,
        out_specs=(P(*WHOLE), P(*WHOLE)),
        check_vma=False,
    )
```

```python
import functools

import jax
import jax.numpy as jnp
from jax import lax
from jax.experimental import pallas as pl
from jax.experimental.pallas import tpu as pltpu
from jax.sharding import PartitionSpec as P

EPSILON = 1e-06
MESH = pl.DeviceIdType.MESH
BF = jnp.bfloat16
F32 = jnp.float32
WHOLE = (("group", "member"), None)
PARTS = 4
OWN, LO, Y1, Y3, LO_Y1, LO_Y3, Y2, LO_Y2 = range(8)


def flip(value, code):
    if code == 0:
        return value
    if code == 1:
        return value + 1 - 2 * (value % 2)
    if code == 2:
        return (value + 2) % 4
    return 3 - value


def peer(x=0, z=0, core=0, lo=0, y=0):
    group, member = lax.axis_index("group"), lax.axis_index("member")
    at_x, at_z, at_core = group // 8, (group // 2) % 4, group % 2
    at_lo, at_y = member // 4, member % 4
    return (
        flip(at_x, x) * 8 + flip(at_z, z) * 2 + flip(at_core, core),
        flip(at_lo, lo) * 4 + flip(at_y, y),
    )


PEERS = (
    dict(core=1),
    dict(x=1),
    dict(x=3),
    dict(x=3, core=1),
    dict(z=1),
    dict(z=3),
    dict(lo=1),
    dict(y=1),
    dict(y=3),
)


def unit_rows(raw):
    values = raw.astype(F32)
    scale = lax.rsqrt(jnp.sum(values * values, axis=-1, keepdims=True) + EPSILON)
    return values * scale, scale


def back_unit(unit, scale, grad):
    return (grad - unit * jnp.sum(unit * grad, axis=-1, keepdims=True)) * scale


def choose(code, zero, one, two, three):
    low = jnp.where(code == 1, one, zero)
    high = jnp.where(code == 3, three, two)
    return jnp.where(code >= 2, high, low)


def scratch(rows, wide):
    piece = rows // PARTS
    half = piece // 2
    unit = pltpu.VMEM((rows, wide), BF)
    both = pltpu.VMEM((2 * half, wide), BF)
    pair = pltpu.VMEM((2 * piece, wide), BF)
    each = lambda ref: [ref] * PARTS
    return dict(
        img=pltpu.VMEM((8 * rows, wide), BF),
        txt=pltpu.VMEM((5 * rows, wide), BF),
        wgt=pltpu.VMEM((5 * rows, 8 * rows), BF),
        bank=each(pltpu.VMEM((8, piece, wide), BF)),
        g_near=each(both),
        g_far=each(both),
        g_s3=each(both),
        g_s21=each(both),
        g_s23=each(both),
        g_r11=each(both),
        g_r13=each(both),
        g_r21=each(both),
        g_r23=each(both),
        d_own=each(pair),
        d_core=each(pair),
        b_near=each(both),
        b_far=each(both),
        b_s3=each(both),
        b_s21=each(both),
        b_s23=each(both),
        b_r11=each(both),
        b_r13=each(both),
        b_r21=each(both),
        b_r23=each(both),
        d31_out=each(pltpu.VMEM((piece, wide), BF)),
        d31_in=each(pltpu.VMEM((piece, wide), BF)),
        z_sum=each(pltpu.VMEM((4, piece, wide), F32)),
        z_s=each(pltpu.VMEM((3, piece, wide), BF)),
        z_out=each(pltpu.VMEM((piece, wide), BF)),
        z_r2=each(pltpu.VMEM((piece, wide), BF)),
        z_r1=each(pltpu.VMEM((piece, wide), BF)),
        z_r3=each(pltpu.VMEM((piece, wide), BF)),
        d_text=pltpu.VMEM((2 * rows, wide), F32),
        d_text_in=pltpu.VMEM((rows, wide), F32),
        d_img=pltpu.VMEM((8 * rows, wide), F32),
        i_s=[unit] * 7,
        i_r=[unit] * 7,
        pic=unit,
        cap=unit,
        mult=pltpu.SMEM((1,), F32),
        off=pltpu.SMEM((1,), F32),
        code=pltpu.SMEM((4,), jnp.int32),
        load=pltpu.SemaphoreType.DMA((5,)),
        scale_u=pltpu.VMEM((rows, 1), F32),
        scale_v=pltpu.VMEM((rows, 1), F32),
        send=pltpu.SemaphoreType.DMA((160,)),
        recv=pltpu.SemaphoreType.DMA((160,)),
    )


def kernel(lite, pic_any, cap_any, mult_any, off_any, code_any, gi_ref, gt_ref, s):
    rows, wide = pic_any.shape
    pic_ref, cap_ref = s["pic"], s["cap"]
    mult_ref, off_ref, code_ref = s["mult"], s["off"], s["code"]
    piece = rows // PARTS
    half = piece // 2
    img, txt, wgt = s["img"], s["txt"], s["wgt"]
    copies, text_seen = {}, []

    def send(name, src, dst, **to):
        at = len(copies)
        copy = pltpu.make_async_remote_copy(
            src_ref=src,
            dst_ref=dst,
            send_sem=s["send"].at[at],
            recv_sem=s["recv"].at[at],
            device_id=peer(**to),
            device_id_type=MESH,
        )
        copies[name] = copy
        copy.start()

    def arrived(*names):
        for name in names:
            copies[name].wait_recv()

    def slot(at):
        return pl.ds(at * rows, rows)

    def part(j):
        return pl.ds(j * piece, piece)

    def text_at(j):
        return 2 * rows + 3 * j * piece

    barrier = pltpu.get_barrier_semaphore()
    for to in PEERS:
        pl.semaphore_signal(barrier, inc=1, device_id=peer(**to), device_id_type=MESH)

    loads = [
        pltpu.make_async_copy(src, dst, s["load"].at[at])
        for at, (src, dst) in enumerate(
            (
                (cap_any, cap_ref),
                (pic_any, pic_ref),
                (mult_any, mult_ref),
                (off_any, off_ref),
                (code_any, code_ref),
            )
        )
    ]
    for load in loads:
        load.start()
    loads[0].wait()
    unit_v, scale_v = unit_rows(cap_ref[...])
    s["scale_v"][...] = scale_v
    own_text = unit_v.astype(BF)
    txt[slot(0), :] = own_text
    for j in range(PARTS):
        s["bank"][j][0] = own_text[j * piece : (j + 1) * piece]
    loads[1].wait()
    unit_u, scale_u = unit_rows(pic_ref[...])
    s["scale_u"][...] = scale_u
    img[slot(OWN), :] = unit_u.astype(BF)
    for load in loads[2:]:
        load.wait()
    mult, off = mult_ref[0], off_ref[0]
    codes = [code_ref[i] for i in range(4)]
    code_a, code_b = jnp.int32(99), jnp.int32(-1)
    for code in codes:
        code_a = jnp.minimum(code_a, jnp.where(code == 1, 99, code))
        code_b = jnp.maximum(code_b, jnp.where(code == 31, -1, code))
    core_of = [code_a & 1, code_b & 1]
    z_of = [(code_a >> 1) & 3, (code_b >> 1) & 3]
    x_of = [(code_a >> 3) & 3, (code_b >> 3) & 3]
    need_1 = (z_of[0] == 1) | (z_of[1] == 1)
    slot_of = [jnp.where(z == 2, 1, z) for z in z_of] if lite else z_of
    pl.semaphore_wait(barrier, len(PEERS))

    def z_first(j):
        src = s["bank"][j].at[0]
        if lite:
            send(f"z3_{j}", src, s["bank"][j].at[3], z=3)
            return
        send(f"z1_{j}", src, s["bank"][j].at[1], z=1)
        send(f"z3_{j}", src, s["bank"][j].at[3], z=3)

    def z_second(j):
        bank = s["bank"][j]
        if lite:
            arrived(f"z3_{j}")
            s["z_out"][j][...] = jnp.where(need_1, bank[0], bank[3])
            send(f"z1_{j}", s["z_out"][j], bank.at[1], z=1)
            send(f"c3_{j}", bank.at[3], bank.at[7], core=1)
            return
        near, far = pl.ds(0, half), pl.ds(half, half)
        arrived(f"z1_{j}")
        send(f"z2a_{j}", bank.at[1, near], bank.at[2, near], z=3)
        arrived(f"z3_{j}")
        send(f"z2b_{j}", bank.at[3, far], bank.at[2, far], z=1)
        send(f"c1_{j}", bank.at[1], bank.at[5], core=1)
        send(f"c3_{j}", bank.at[3], bank.at[7], core=1)

    def fetch_31(j):
        bank = s["bank"][j]
        send(f"t31_{j}", bank.at[3], txt.at[pl.ds(text_at(j), piece)], x=3, core=1)

    def z_done(j):
        bank = s["bank"][j]
        if lite:
            arrived(f"z1_{j}")
            send(f"c1_{j}", bank.at[1], bank.at[5], core=1)
            return
        arrived(f"z2a_{j}", f"z2b_{j}")
        send(f"c2_{j}", bank.at[2], bank.at[6], core=1)

    def x_send(tag, j, far, where):
        near_ref, far_ref, s3 = s[tag + "near"][j], s[tag + "far"][j], s[tag + "s3"][j]
        send(f"{tag}11_{j}", near_ref, s[tag + "r11"][j], x=1)
        for m in range(2):
            at = pl.ds(m * half, half)
            s3[at, :] = jnp.where(x_of[m] == 2, far_ref[at, :], near_ref[at, :])
        send(f"{tag}13_{j}", s3, s[tag + "r13"][j], x=3)

    def x_second(tag, j):
        far_ref = s[tag + "far"][j]
        for side, name in ((3, "11"), (1, "13")):
            arrived(f"{tag}{name}_{j}")
            got, out = s[f"{tag}r{name}"][j], s[f"{tag}s2{side}"][j]
            for m in range(2):
                at = pl.ds(m * half, half)
                out[at, :] = jnp.where(x_of[m] == 2, got[at, :], far_ref[at, :])
            send(f"{tag}2{side}_{j}", out, s[f"{tag}r2{side}"][j], x=side)

    def x_done(tag, j, m):
        at = pl.ds(m * half, half)
        r11, r13, r21, r23 = (s[f"{tag}r{n}"][j][at, :] for n in ("11", "13", "21", "23"))
        near = choose(x_of[m], s[tag + "near"][j][at, :], r11, r23, r13)
        far = choose(x_of[m], s[tag + "far"][j][at, :], r21, r21, r23)
        return near, far

    def x_text(j):
        bank = s["bank"][j]
        arrived(f"c1_{j}", f"c3_{j}")
        if not lite:
            arrived(f"c2_{j}")
        for m in range(2):
            at = pl.ds(m * half, half)
            picked = bank[core_of[m] * 4 + slot_of[m]]
            s["g_near"][j][at, :] = picked[:half]
            s["g_far"][j][at, :] = picked[half:]
        x_send("g_", j, None, None)

    def text_in(j):
        arrived(f"g_21_{j}", f"g_23_{j}")
        for m in range(2):
            near, far = x_done("g_", j, m)
            base = text_at(j) + (1 + m) * piece
            txt[pl.ds(base, half), :] = near
            txt[pl.ds(base + half, half), :] = far

    def weigh(start, count, at, wide_by, positive=False):
        cols = pl.ds(at * rows, wide_by * rows)
        logits = lax.dot_general(
            txt[pl.ds(start, count), :],
            img[cols, :],
            (((1,), (1,)), ((), ())),
            preferred_element_type=F32,
        )
        factor = jax.nn.sigmoid(mult * logits + off)
        if positive:
            row = lax.broadcasted_iota(jnp.int32, factor.shape, 0)
            col = lax.broadcasted_iota(jnp.int32, factor.shape, 1)
            factor = factor - jnp.where((row == col) & (row < rows), 1.0, 0.0)
        wgt[pl.ds(start, count), cols] = (mult * factor).astype(BF)

    def text_grad(start, count):
        return jnp.dot(wgt[pl.ds(start, count), :], img[...], preferred_element_type=F32)

    def image_grad(start, count, at):
        cols = pl.ds(at * rows, 2 * rows)
        return lax.dot_general(
            wgt[pl.ds(start, count), cols],
            txt[pl.ds(start, count), :],
            (((0,), (0,)), ((), ())),
            preferred_element_type=F32,
        )

    def weigh_in(j):
        arrived(f"t31_{j}")
        weigh(text_at(j), 3 * piece, 0, 8)

    def grads_out(j):
        grad = text_grad(text_at(j), 3 * piece).astype(BF)
        s["d_own"][j][...] = grad[piece:]
        send(f"dc_{j}", s["d_own"][j], s["d_core"][j], core=1)
        s["d31_out"][j][...] = grad[:piece]

    def send_31(j):
        send(f"d31_{j}", s["d31_out"][j], s["d31_in"][j], x=3, core=1)

    def grads_x(j):
        arrived(f"dc_{j}")
        own, other = s["d_own"][j], s["d_core"][j]
        for m in range(2):
            at = pl.ds(m * half, half)
            for name, base in (("near", m * piece), ("far", m * piece + half)):
                take = pl.ds(base, half)
                s["b_" + name][j][at, :] = jnp.where(core_of[m] == 1, other[take, :], own[take, :])
        x_send("b_", j, None, None)

    def grads_z(j):
        arrived(f"b_21_{j}", f"b_23_{j}", f"d31_{j}")
        total = s["z_sum"][j]
        zero = jnp.zeros((half, wide), F32)
        got = [x_done("b_", j, m) for m in range(2)]
        for h in range(2):
            at = pl.ds(h * half, half)
            a, b = got[0][h].astype(F32), got[1][h].astype(F32)
            for k in (0, 1, 3) if lite else range(4):
                to_k = [slot == k for slot in slot_of]
                value = jnp.where(to_k[0], a, zero) + jnp.where(to_k[1], b, zero)
                if k == 3:
                    value = value + s["d31_in"][j][at, :].astype(F32)
                total[k, at, :] = value
        out = s["z_s"][j]
        if lite:
            out[1] = total[1].astype(BF)
            send(f"dz1_{j}", out.at[1], s["z_r1"][j], z=1)
            return
        out[0] = total[2].astype(BF)
        near, far = pl.ds(0, half), pl.ds(half, half)
        send(f"dz2a_{j}", out.at[0, near], s["z_r2"][j].at[near], z=3)
        send(f"dz2b_{j}", out.at[0, far], s["z_r2"][j].at[far], z=1)

    def grads_z_second(j):
        total, out, got = s["z_sum"][j], s["z_s"][j], s["z_r2"][j]
        if lite:
            arrived(f"dz1_{j}")
            came = s["z_r1"][j][...].astype(F32)
            zero = jnp.zeros_like(came)
            out[2] = (total[3] + jnp.where(need_1, zero, came)).astype(BF)
            send(f"dz3_{j}", out.at[2], s["z_r3"][j], z=3)
            total[0] = total[0] + jnp.where(need_1, came, zero)
            return
        near, far = pl.ds(0, half), pl.ds(half, half)
        arrived(f"dz2a_{j}")
        out[1, far, :] = total[1, far, :].astype(BF)
        out[1, near, :] = (total[1, near, :] + got[near, :].astype(F32)).astype(BF)
        send(f"dz1_{j}", out.at[1], s["z_r1"][j], z=1)
        arrived(f"dz2b_{j}")
        out[2, near, :] = total[3, near, :].astype(BF)
        out[2, far, :] = (total[3, far, :] + got[far, :].astype(F32)).astype(BF)
        send(f"dz3_{j}", out.at[2], s["z_r3"][j], z=3)

    def text_out(j):
        arrived(f"dz3_{j}")
        if not text_seen:
            text_seen.append(j)
            arrived("d1")
        total = s["z_sum"][j][0] + s["z_r3"][j][...].astype(F32)
        if not lite:
            arrived(f"dz1_{j}")
            total = total + s["z_r1"][j][...].astype(F32)
        total = total + s["d_text"][part(j), :] + s["d_text_in"][part(j), :]
        scale = s["scale_v"][part(j), :]
        unit = cap_ref[part(j), :].astype(F32) * scale
        gt_ref[part(j), :] = back_unit(unit, scale, total)

    def early(at):
        weigh(0, 2 * rows, at, 2, at == OWN)
        s["d_img"][pl.ds(at * rows, 2 * rows), :] = image_grad(0, 2 * rows, at)

    def early_text():
        s["d_text"][...] = text_grad(0, 2 * rows)
        send("d1", s["d_text"].at[slot(1)], s["d_text_in"], core=1)

    def late_image(at):
        here = pl.ds(at * rows, 2 * rows)
        s["d_img"][here, :] = s["d_img"][here, :] + image_grad(2 * rows, 3 * rows, at)

    def half_send(name, n, at, adds, h, **to):
        arrived(*(f"{add}_{h}" for add, _ in adds))
        here = pl.ds(h * rows // 2, rows // 2)
        value = s["d_img"][pl.ds(at * rows + h * rows // 2, rows // 2), :]
        for _, m in adds:
            value = value + s["i_r"][m][here, :].astype(F32)
        s["i_s"][n][here, :] = value.astype(BF)
        send(f"{name}_{h}", s["i_s"][n].at[here], s["i_r"][n].at[here], **to)

    def image_first():
        late_image(Y2)
        for h in range(2):
            half_send("u7", 0, LO_Y2, [], h, y=1)
            half_send("u6", 1, Y2, [], h, y=3)

    def image_lo_y1():
        late_image(LO_Y1)
        for h in range(2):
            half_send("u4", 2, LO_Y1, [], h, y=1)

    def image_u5(h):
        half_send("u5", 4, LO_Y3, [("u7", 0)], h, y=3)

    def image_u3(h):
        half_send("u3", 3, Y3, [], h, y=3)

    def image_u2(h):
        half_send("u2", 5, Y1, [("u6", 1)], h, y=1)

    def image_ul(h):
        half_send("ul", 6, LO, [("u4", 2), ("u5", 4)], h, lo=1)

    def image_out(h):
        arrived(*(f"{name}_{h}" for name in ("u2", "u3", "ul")))
        here = pl.ds(h * rows // 2, rows // 2)
        total = s["d_img"][here, :]
        for m in (5, 3, 6):
            total = total + s["i_r"][m][here, :].astype(F32)
        scale = s["scale_u"][here, :]
        unit = pic_ref[here, :].astype(F32) * scale
        gi_ref[here, :] = back_unit(unit, scale, total)

    def pass_image(name, source, target, h, **to):
        here = pl.ds(h * rows // 2, rows // 2)
        at = lambda n: img.at[pl.ds(n * rows + h * rows // 2, rows // 2)]
        send(f"{name}_{h}", at(source), at(target), **to)

    def start_lo(h):
        pass_image("l", OWN, LO, h, lo=1)

    def start():
        for h in range(2):
            pass_image("y1", OWN, Y1, h, y=1)
            pass_image("y3", OWN, Y3, h, y=3)
        send("t1", txt.at[slot(0)], txt.at[slot(1)], core=1)

    def other_core():
        arrived("t1")
        for j in range(PARTS):
            s["bank"][j][4] = txt[pl.ds(rows + j * piece, piece), :]

    def img_lo(h):
        arrived(f"l_{h}")
        pass_image("ly3", LO, LO_Y3, h, y=3)
        pass_image("ly1", LO, LO_Y1, h, y=1)

    def img_y2(h):
        arrived(f"y1_{h}")
        pass_image("y2", Y1, Y2, h, y=3)

    def img_lo_y2(h):
        arrived(f"ly3_{h}")
        pass_image("ly2", LO_Y3, LO_Y2, h, y=1)

    def early_own():
        early(OWN)

    def early_y1():
        arrived("y3_0", "y3_1")
        early(Y1)

    def early_lo():
        arrived("ly1_0", "ly1_1")
        early(LO_Y1)

    def early_y2():
        arrived("y2_0", "y2_1", "ly2_0", "ly2_1")
        early(Y2)

    if lite:
        steps = [
            start,
            (z_first, 0),
            (z_first, 1),
            (start_lo, 0),
            other_core,
            (z_second, 0),
            (fetch_31, 0),
            (z_first, 2),
            (start_lo, 1),
            (img_lo, 0),
            (z_second, 1),
            (fetch_31, 1),
            (img_y2, 0),
            (z_done, 0),
            (x_text, 0),
            (z_second, 2),
            (img_lo_y2, 0),
            (z_done, 1),
            (z_first, 3),
            (img_lo, 1),
            (img_y2, 1),
            (x_text, 1),
            (x_second, "g_", 0),
            (z_done, 2),
            (z_second, 3),
            (x_second, "g_", 1),
            (img_lo_y2, 1),
            (x_text, 2),
            early_own,
            early_lo,
            (text_in, 0),
            (text_in, 1),
            (fetch_31, 2),
            early_y1,
            (z_done, 3),
            (x_second, "g_", 2),
            early_y2,
            (weigh_in, 0),
            (x_text, 3),
            (grads_out, 0),
            (weigh_in, 1),
            (fetch_31, 3),
            (grads_out, 1),
            (grads_x, 0),
            (send_31, 0),
            (x_second, "g_", 3),
            (text_in, 2),
            early_text,
            (weigh_in, 2),
            (grads_x, 1),
            (x_second, "b_", 0),
            (grads_out, 2),
            (text_in, 3),
            (weigh_in, 3),
            image_first,
            (send_31, 1),
            (grads_out, 3),
            (x_second, "b_", 1),
            (grads_x, 2),
            image_lo_y1,
            (grads_z, 0),
            (grads_z, 1),
            (send_31, 2),
            (x_second, "b_", 2),
            (late_image, Y1),
            (late_image, OWN),
            (grads_z_second, 0),
            (grads_x, 3),
            (image_u5, 0),
            (grads_z, 2),
            (send_31, 3),
            (grads_z_second, 1),
            (image_u2, 1),
            (x_second, "b_", 3),
            (image_u2, 0),
            (image_u5, 1),
            (image_u3, 0),
            (image_ul, 0),
            (grads_z, 3),
            (image_ul, 1),
            (text_out, 0),
            (grads_z_second, 2),
            (image_u3, 1),
            (image_out, 0),
            (text_out, 1),
            (grads_z_second, 3),
            (text_out, 2),
            (text_out, 3),
            (image_out, 1),
        ]
    else:
        steps = [
            start,
            (start_lo, 0),
            (z_first, 0),
            (img_y2, 0),
            (start_lo, 1),
            other_core,
            (z_second, 0),
            (img_lo, 0),
            (z_done, 0),
            (z_first, 2),
            (x_text, 0),
            (img_lo, 1),
            (fetch_31, 0),
            (img_y2, 1),
            (z_first, 1),
            early_y1,
            (z_second, 2),
            (x_second, "g_", 0),
            (img_lo_y2, 1),
            (img_lo_y2, 0),
            (z_second, 1),
            (z_done, 2),
            (z_first, 3),
            (fetch_31, 1),
            (x_text, 2),
            early_lo,
            (z_done, 1),
            early_own,
            (fetch_31, 2),
            (text_in, 0),
            (x_text, 1),
            early_y2,
            (x_second, "g_", 2),
            (weigh_in, 0),
            (grads_out, 0),
            (z_second, 3),
            (send_31, 0),
            (x_second, "g_", 1),
            (z_done, 3),
            (grads_x, 0),
            (text_in, 2),
            (x_text, 3),
            (weigh_in, 2),
            (text_in, 1),
            (grads_out, 2),
            (fetch_31, 3),
            (weigh_in, 1),
            (x_second, "b_", 0),
            (grads_x, 2),
            (grads_out, 1),
            early_text,
            (x_second, "g_", 3),
            (grads_x, 1),
            (x_second, "b_", 2),
            (grads_z, 0),
            (send_31, 2),
            (text_in, 3),
            (weigh_in, 3),
            (send_31, 1),
            image_first,
            (grads_out, 3),
            (grads_z_second, 0),
            (x_second, "b_", 1),
            (grads_x, 3),
            image_lo_y1,
            (grads_z, 2),
            (grads_z, 1),
            (image_u5, 0),
            (grads_z_second, 2),
            (image_u5, 1),
            (send_31, 3),
            (late_image, Y1),
            (x_second, "b_", 3),
            (late_image, OWN),
            (grads_z_second, 1),
            (image_u2, 0),
            (image_u3, 0),
            (grads_z, 3),
            (image_u3, 1),
            (image_u2, 1),
            (image_ul, 0),
            (text_out, 0),
            (grads_z_second, 3),
            (image_out, 0),
            (image_ul, 1),
            (text_out, 1),
            (text_out, 2),
            (text_out, 3),
            (image_out, 1),
        ]
    for step in steps:
        if isinstance(step, tuple):
            step[0](*step[1:])
        else:
            step()
    for copy in copies.values():
        copy.wait_send()


def call(lite, *args):
    rows, wide = args[0].shape
    in_vmem = pl.BlockSpec(memory_space=pltpu.VMEM)
    anywhere = pl.BlockSpec(memory_space=pl.ANY)
    out = jax.ShapeDtypeStruct((rows, wide), F32)
    return pl.pallas_call(
        functools.partial(kernel, lite),
        out_shape=(out, out),
        in_specs=[anywhere] * 5,
        out_specs=(in_vmem, in_vmem),
        scratch_shapes=[scratch(rows, wide)],
        compiler_params=pltpu.CompilerParams(
            collective_id=0 if lite else 1, has_side_effects=True, vmem_limit_bytes=38 << 20
        ),
        name="contrastive_lite" if lite else "contrastive_full",
    )(*args)


def local(*args):
    z_codes = (args[4] >> 1) & 3
    asked = jnp.where(z_codes == 1, 1, jnp.where(z_codes == 2, 2, 0))
    both = lax.reduce(asked, jnp.int32(0), lax.bitwise_or, (0,)) == 3
    return lax.cond(both, functools.partial(call, False), functools.partial(call, True), *args)


def solution(mesh):
    placed = (P(*WHOLE), P(*WHOLE), P(), P(), P())
    return jax.shard_map(
        local,
        mesh=mesh,
        in_specs=placed,
        out_specs=(P(*WHOLE), P(*WHOLE)),
        check_vma=False,
    )
```
